256 devices in a mesh: lon: 16 (over y, x_lo, core), lat: 16 (over x_hi, z).
Axes of the slice: x: 4 (x_hi: 2, x_lo: 2; x = x_hi * 2 + x_lo), y: 4, z: 8, core: 2. Of those that a mesh axis runs over, the one named last changes fastest.
Arguments:
- fields: bfloat16 [1024, 64, 512], P('lon', 'lat'), may hold values from -12 to 12
- in_weight: bfloat16 [512, 1536], replicated, may hold values from -1 to 1
- out_weight: bfloat16 [512, 512], replicated, may hold values from -0.25 to 0.25
- cotangent: bfloat16 [1024, 64, 512], P('lon', 'lat'), may hold values from -6 to 6
Outputs:
- grad_fields: bfloat16 [1024, 64, 512], P('lon', 'lat')
The draws below stay inside these ranges and needn't reach their ends.
All inputs are finite; a program needn't handle non-finite values.
Results may differ from the reference program's by a relative error of at most 0.034.
Values may be sent and summed in bfloat16 or wider, within the bound.
A program may use at most 128 MiB of HBM per device.

```python
import math
import jax
import jax.numpy as jnp
from jax import lax

D = 512
HEADS = 8
LON = 1024
LAT = 64


def draw_fields(key, part):
    key = jax.random.fold_in(key, 11)
    first = jax.random.fold_in(key, 0)
    values = jnp.clip(jax.random.normal(first, (LON, LAT, D), jnp.float32) * 1.5, -6.0, 6.0)
    return values.astype(jnp.bfloat16)


def draw_in_weight(key, part):
    key = jax.random.fold_in(key, 23)
    values = jnp.clip(jax.random.normal(key, (D, 3 * D), jnp.float32), -4.0, 4.0) * D ** (-0.5)
    return values.astype(jnp.bfloat16)


def block_scale(key, shape, pieces, smallest, top_value):
    def one(axis_at, parts):
        steps = jax.random.uniform(jax.random.fold_in(jax.random.fold_in(key, 6), axis_at), (parts,), jnp.float32, smallest / len(pieces), top_value / len(pieces))
        return jnp.repeat(jnp.exp(steps), shape[axis_at] // parts).reshape((-1,) + (1,) * (len(shape) - axis_at - 1))

    loudness = one(*pieces[0])
    for cut in pieces[1:]:
        loudness = loudness * one(*cut)
    return loudness


def centred(key, dims, scale, limit, cuts=(), kind=jnp.bfloat16):
    drawn = jax.random.normal(key, dims, jnp.float32) * scale
    if len(cuts) > 0:
        drawn = block_scale(key, dims, cuts, -0.22, 0.18) * drawn
    return jnp.clip(drawn, min=-limit, max=limit).astype(kind)


def setup_inputs(seed: int = 0) -> dict:
    seeds = jax.random.split(jax.random.key(seed), 5)
    fields = draw_fields(jax.random.fold_in(seeds[4], 71), 0)
    in_weight = draw_in_weight(jax.random.fold_in(seeds[4], 71), 0)
    out_weight = centred(seeds[2], (D, D), D ** -0.5, 0.25)
    cotangent = centred(seeds[3], (LON, LAT, D), 1.0, 6.0, ((0, 16), (1, 16)))
    return {"fields": fields, "in_weight": in_weight, "out_weight": out_weight, "cotangent": cotangent}


def attention_grads(query, keys, values, grad_out, temper):
    query_f = query.astype(jnp.float32)
    keys_f = keys.astype(jnp.float32)
    values_f = values.astype(jnp.float32)
    grad_f = grad_out.astype(jnp.float32)
    scores = jnp.einsum('bshe,bthe->bhst', query_f, keys_f) * temper
    maxima = lax.optimization_barrier(jnp.max(scores, axis=-1, keepdims=True))
    expos = jnp.exp(scores - maxima)
    totals = lax.optimization_barrier(jnp.sum(expos, axis=-1, keepdims=True))
    weights = expos / totals
    weights_bf = lax.optimization_barrier(weights.astype(jnp.bfloat16)).astype(jnp.float32)
    output = jnp.einsum('bhst,bthe->bshe', weights_bf, values_f).astype(jnp.bfloat16)
    deltas = jnp.einsum('bshe,bshe->bhs', grad_f, output.astype(jnp.float32))
    grad_prob = jnp.einsum('bshe,bthe->bhst', grad_f, values_f)
    grad_score = lax.optimization_barrier((weights * (grad_prob - deltas[..., None])).astype(jnp.bfloat16)).astype(jnp.float32)
    grad_query = jnp.einsum('bhst,bthe->bshe', grad_score, keys_f) * temper
    grad_key = jnp.einsum('bhst,bshe->bthe', grad_score, query_f) * temper
    grad_value = jnp.einsum('bhst,bshe->bthe', weights_bf, grad_f)
    return (grad_query, grad_key, grad_value)

def reference(fields, in_weight, out_weight, cotangent):
    half_width = D // 2
    part_heads = HEADS // 2
    head_size = D // HEADS
    temper = 1.0 / math.sqrt(head_size)
    qkv = jnp.dot(fields.reshape(-1, D), in_weight, preferred_element_type=jnp.float32)
    qkv = qkv.astype(jnp.bfloat16).reshape(LON, LAT, 3 * D)
    grad_attn = jnp.dot(cotangent.reshape(-1, D), out_weight.T, preferred_element_type=jnp.float32)
    grad_attn = grad_attn.astype(jnp.bfloat16).reshape(LON, LAT, D)

    def pick(array, offset):
        return array[..., offset:offset + half_width].reshape(LON, LAT, part_heads, head_size)

    def one_sequence(items):
        results = attention_grads(items[0][None], items[1][None], items[2][None], items[3][None], temper)
        return tuple((entry[0] for entry in results))
    row_items = tuple((pick(array, offset).transpose(1, 0, 2, 3) for array, offset in ((qkv, 0), (qkv, D), (qkv, 2 * D), (grad_attn, 0))))
    row_grads = lax.map(one_sequence, row_items)
    row_grads = [entry.transpose(1, 0, 2, 3).reshape(LON, LAT, half_width) for entry in row_grads]
    col_items = tuple((pick(array, offset) for array, offset in ((qkv, half_width), (qkv, D + half_width), (qkv, 2 * D + half_width), (grad_attn, half_width))))
    col_grads = lax.map(one_sequence, col_items)
    col_grads = [entry.reshape(LON, LAT, half_width) for entry in col_grads]
    grad_qkv = jnp.concatenate([row_grads[0], col_grads[0], row_grads[1], col_grads[1], row_grads[2], col_grads[2]], axis=-1)
    grad_qkv = grad_qkv.astype(jnp.bfloat16)
    grad_fields = jnp.dot(grad_qkv.reshape(-1, 3 * D), in_weight.T, preferred_element_type=jnp.float32)
    return grad_fields.astype(jnp.bfloat16).reshape(LON, LAT, D)
```

```python
import math

import jax
import jax.numpy as jnp
from jax import lax
from jax.experimental import pallas as pl
from jax.experimental.pallas import tpu as pltpu
from jax.sharding import PartitionSpec as P

MESH = pl.DeviceIdType.MESH
BF = jnp.bfloat16
F32 = jnp.float32
NT = (((1,), (1,)), ((), ()))
NN = (((1,), (0,)), ((), ()))
TEMPER = 0.125
EXP_SCALE = TEMPER * math.log2(math.e)
GROUP = 16


def dot(a, b, dims=NN):
    return lax.dot_general(a, b, dims, preferred_element_type=F32)


def lat_partner(k, lat):
    i = k // 2
    dz = 4 + (1 - 2 * (i % 2)) * ((i + 1) // 2)
    dx = 1 - k % 2
    return ((lat // 8 + dx) % 2) * 8 + (lat % 8 + dz) % 8


def lon_partner(k, lon):
    i = k // 4
    dy = 2 + (1 - 2 * (i % 2)) * ((i + 1) // 2)
    dx = 1 - (k // 2) % 2
    dc = 1 - k % 2
    return ((lon // 4 + dy) % 4) * 4 + (((lon // 2) % 2 + dx) % 2) * 2 + (lon % 2 + dc) % 2


def kernel(
    x_hbm, w_hbm, wo_hbm, c_hbm, out_ref,
    x, w, wo, cot, gcol, perm, wkv,
    skv, sqg, rkv, rqg, kvt, dkv, sendkv, sendq, retkv, retq,
    cx, cg, cq, ck, cv, cgt, cdq, cdk, cdv, cpart, cret,
    in_sem, own_sem, fs, fr, gs, gr, ks, kr, qs, qr, cs, cr, ds_, dr, es, er,
):
    lon = lax.axis_index("lon")
    lat = lax.axis_index("lat")
    my_l = lon // 4
    my_h = lon % 4

    loads = [
        pltpu.make_async_copy(src, dst, in_sem.at[i])
        for i, (src, dst) in enumerate(((x_hbm, x), (c_hbm, cot), (wo_hbm, wo), (w_hbm, w)))
    ]
    for load in loads:
        load.start()

    barrier = pltpu.get_barrier_semaphore()

    @pl.loop(0, GROUP - 1)
    def _(k):
        pl.semaphore_signal(
            barrier, inc=1, device_id=(lon, lat_partner(k, lat)), device_id_type=MESH
        )
        pl.semaphore_signal(
            barrier, inc=1, device_id=(lon_partner(k, lon), lat), device_id_type=MESH
        )

    def to_lat(k, src, dst, ssem, rsem):
        p = lat_partner(k, lat)
        return pltpu.make_async_remote_copy(
            src_ref=src.at[pl.ds(p * 16, 16)],
            dst_ref=dst.at[pl.ds(lat * 16, 16)],
            send_sem=ssem.at[p],
            recv_sem=rsem.at[lat],
            device_id=(lon, p),
            device_id_type=MESH,
        )

    def from_lat(k, src, dst, ssem, rsem):
        p = lat_partner(k, lat)
        return pltpu.make_async_remote_copy(
            src_ref=src.at[pl.ds(p * 16, 16)],
            dst_ref=dst.at[pl.ds(p * 16, 16)],
            send_sem=ssem.at[p],
            recv_sem=rsem.at[p],
            device_id=(lon, p),
            device_id_type=MESH,
        )

    def to_task(k, src, dst, ssem, rsem):
        p = lon_partner(k, lon)
        return pltpu.make_async_remote_copy(
            src_ref=src.at[p % 4, pl.ds((p // 4) * 64, 64)],
            dst_ref=dst.at[pl.ds(lon * 64, 64)],
            send_sem=ssem.at[p],
            recv_sem=rsem.at[lon],
            device_id=(p, lat),
            device_id_type=MESH,
        )

    def from_task(k, src, dst, ssem, rsem):
        p = lon_partner(k, lon)
        return pltpu.make_async_remote_copy(
            src_ref=src.at[p % 4, pl.ds((p // 4) * 64, 64)],
            dst_ref=dst.at[pl.ds(p * 64, 64)],
            send_sem=ssem.at[p],
            recv_sem=rsem.at[p],
            device_id=(p, lat),
            device_id_type=MESH,
        )

    def back_task(k, src, dst, ssem, rsem):
        p = lon_partner(k, lon)
        return pltpu.make_async_remote_copy(
            src_ref=src.at[pl.ds(p * 64, 64)],
            dst_ref=dst.at[my_h, pl.ds(my_l * 64, 64)],
            send_sem=ssem.at[p],
            recv_sem=rsem.at[lon],
            device_id=(p, lat),
            device_id_type=MESH,
        )

    def home_task(k, src, dst, ssem, rsem):
        p = lon_partner(k, lon)
        return pltpu.make_async_remote_copy(
            src_ref=src.at[pl.ds(p * 64, 64)],
            dst_ref=dst.at[p % 4, pl.ds((p // 4) * 64, 64)],
            send_sem=ssem.at[p],
            recv_sem=rsem.at[p],
            device_id=(p, lat),
            device_id_type=MESH,
        )

    def start_all(make, *args):
        @pl.loop(0, GROUP - 1)
        def _(k):
            make(k, *args).start()

    def wait_recv(make, *args):
        @pl.loop(0, GROUP - 1)
        def _(k):
            make(k, *args).wait_recv()

    def wait_send(make, *args):
        @pl.loop(0, GROUP - 1)
        def _(k):
            make(k, *args).wait_send()

    row = lax.broadcasted_iota(jnp.int32, (256, 256), 0)
    col = lax.broadcasted_iota(jnp.int32, (256, 256), 1)
    perm[...] = jnp.where(col == (row % 64) * 4 + row // 64, 1.0, 0.0).astype(BF)

    loads[0].wait()
    pl.semaphore_wait(barrier, 2 * (GROUP - 1))

    start_all(to_lat, x, cx, fs, fr)

    loads[1].wait()
    loads[2].wait()
    g = dot(cot[...], wo[...], NT).astype(BF)
    gcol[...] = g[:, 256:]
    start_all(to_lat, gcol, cg, gs, gr)

    loads[3].wait()
    for h in range(4):
        wkv[:, h * 128 : h * 128 + 64] = w[:, 512 + h * 64 : 576 + h * 64]
        wkv[:, h * 128 + 64 : h * 128 + 128] = w[:, 1024 + h * 64 : 1088 + h * 64]
    xp = dot(perm[...], x[...]).astype(BF)
    kv = dot(xp, wkv[...]).astype(BF)
    for h in range(4):
        skv[h] = kv[:, h * 128 : h * 128 + 128]
    start_all(to_task, skv, rkv, ks, kr)
    gp_row = dot(perm[...], g[:, :256])
    q = dot(xp, w[:, :256])
    for h in range(4):
        sqg[h] = jnp.concatenate(
            [q[:, h * 64 : h * 64 + 64], gp_row[:, h * 64 : h * 64 + 64]], axis=1
        ).astype(BF)
    start_all(to_task, sqg, rqg, qs, qr)

    own = [
        pltpu.make_async_copy(
            skv.at[my_h, pl.ds(my_l * 64, 64)], rkv.at[pl.ds(lon * 64, 64)], own_sem.at[0]
        ),
        pltpu.make_async_copy(
            sqg.at[my_h, pl.ds(my_l * 64, 64)], rqg.at[pl.ds(lon * 64, 64)], own_sem.at[1]
        ),
        pltpu.make_async_copy(
            x.at[pl.ds(lat * 16, 16)], cx.at[pl.ds(lat * 16, 16)], own_sem.at[2]
        ),
        pltpu.make_async_copy(
            gcol.at[pl.ds(lat * 16, 16)], cg.at[pl.ds(lat * 16, 16)], own_sem.at[3]
        ),
    ]
    for copy in own:
        copy.start()

    own[2].wait()
    wait_recv(from_lat, x, cx, fs, fr)
    cxv = cx[...]
    for t in range(2):
        cq[t] = dot(cxv, w[:, 256 + t * 128 : 384 + t * 128]).astype(BF)
        ck[t] = dot(cxv, w[:, 768 + t * 128 : 896 + t * 128]).astype(BF)
        cv[t] = dot(cxv, w[:, 1280 + t * 128 : 1408 + t * 128]).astype(BF)
    own[3].wait()
    wait_recv(from_lat, gcol, cg, gs, gr)
    for t in range(2):
        cgt[t] = cg[:, t * 128 : t * 128 + 128]
    cdq[...] = jnp.zeros_like(cdq)
    cdk[...] = jnp.zeros_like(cdk)
    cdv[...] = jnp.zeros_like(cdv)
    same = (row // 4) % 4 == (col // 4) % 4
    lane = lax.broadcasted_iota(jnp.int32, (256, 128), 1)

    @pl.loop(0, 4)
    def _(h):
        t = h // 2
        mine = lane // 64 == h % 2

        def keep(a):
            return jnp.where(mine, a.astype(F32), 0.0).astype(BF)

        qz = keep(cq[t])
        kz = keep(ck[t])
        gz = keep(cgt[t])
        st = jnp.where(same, dot(ck[t], qz, NT), -1e30)
        gp = dot(cv[t], gz, NT)
        top = jnp.max(st, axis=0, keepdims=True)
        p = jnp.exp2((st - top) * EXP_SCALE)
        inv = 1.0 / jnp.sum(p, axis=0, keepdims=True)
        delta = jnp.sum(p * gp, axis=0, keepdims=True) * inv
        weights = p * inv
        ds = (weights * (gp - delta)).astype(BF)
        cdk[t] += dot(ds, qz)
        cdv[t] += dot(weights.astype(BF), gz)
        cdq[t] += lax.dot_general(ds, kz, (((0,), (0,)), ((), ())), preferred_element_type=F32)

    part = jnp.zeros((256, 512), F32)
    for t in range(2):
        part += dot((cdq[t] * TEMPER).astype(BF), w[:, 256 + t * 128 : 384 + t * 128], NT)
        part += dot((cdk[t] * TEMPER).astype(BF), w[:, 768 + t * 128 : 896 + t * 128], NT)
        part += dot(cdv[t].astype(BF), w[:, 1280 + t * 128 : 1408 + t * 128], NT)
    cpart[...] = part.astype(BF)
    start_all(to_lat, cpart, cret, cs, cr)
    own_part = pltpu.make_async_copy(
        cpart.at[pl.ds(lat * 16, 16)], cret.at[pl.ds(lat * 16, 16)], own_sem.at[2]
    )
    own_part.start()

    own[0].wait()
    wait_recv(from_task, skv, rkv, ks, kr)
    kvt[...] = rkv[...].astype(F32).T.astype(BF)
    own[1].wait()
    wait_recv(from_task, sqg, rqg, qs, qr)
    dkv[...] = jnp.zeros_like(dkv)

    @pl.loop(0, 4)
    def _(c):
        rows = pl.ds(pl.multiple_of(c * 256, 256), 256)
        qg = rqg[rows, :].astype(F32)
        qz = jnp.where(lane < 64, qg, 0.0).astype(BF)
        gz = jnp.where(lane < 64, 0.0, qg).astype(BF)
        st = dot(rkv[...], qz, NT)
        gp = dot(rkv[...], gz, NT)
        top = jnp.max(st, axis=0, keepdims=True)
        p = jnp.exp2((st - top) * EXP_SCALE)
        inv = 1.0 / jnp.sum(p, axis=0, keepdims=True)
        delta = jnp.sum(p * gp, axis=0, keepdims=True) * inv
        weights = p * inv
        ds = (weights * (gp - delta)).astype(BF)
        dkv[...] += dot(ds, qz) + dot(weights.astype(BF), gz)
        dqt = dot(kvt[...], ds)
        sendq[rows, :] = (dqt.T * TEMPER).astype(BF)

    lane_all = lax.broadcasted_iota(jnp.int32, (1024, 128), 1)
    sendkv[...] = (dkv[...] * jnp.where(lane_all < 64, TEMPER, 1.0)).astype(BF)
    start_all(back_task, sendq, retq, ds_, dr)
    start_all(back_task, sendkv, retkv, es, er)
    own_back = [
        pltpu.make_async_copy(
            sendq.at[pl.ds(lon * 64, 64)], retq.at[my_h, pl.ds(my_l * 64, 64)], own_sem.at[0]
        ),
        pltpu.make_async_copy(
            sendkv.at[pl.ds(lon * 64, 64)], retkv.at[my_h, pl.ds(my_l * 64, 64)], own_sem.at[1]
        ),
    ]
    for copy in own_back:
        copy.start()

    own_back[0].wait()
    wait_recv(home_task, sendq, retq, ds_, dr)
    rp = jnp.zeros((256, 512), F32)
    for h in range(4):
        rp += dot(retq[h][:, :64], w[:, h * 64 : h * 64 + 64], NT)
    own_back[1].wait()
    wait_recv(home_task, sendkv, retkv, es, er)
    for h in range(4):
        rp += dot(retkv[h], wkv[:, h * 128 : h * 128 + 128], NT)
    home = lax.dot_general(
        perm[...], rp.astype(BF), (((0,), (0,)), ((), ())), preferred_element_type=F32
    )
    own_part.wait()
    wait_recv(from_lat, cpart, cret, cs, cr)
    out_ref[...] = (home + cret[...].astype(F32)).astype(BF)

    wait_send(to_lat, x, cx, fs, fr)
    wait_send(to_lat, gcol, cg, gs, gr)
    wait_send(to_task, skv, rkv, ks, kr)
    wait_send(to_task, sqg, rqg, qs, qr)
    wait_send(to_lat, cpart, cret, cs, cr)
    wait_send(back_task, sendq, retq, ds_, dr)
    wait_send(back_task, sendkv, retkv, es, er)


def per_device(fields, in_weight, out_weight, cotangent):
    shape = fields.shape

    def vm(*dims, dtype=BF):
        return pltpu.VMEM(dims, dtype)

    out = pl.pallas_call(
        kernel,
        out_shape=jax.ShapeDtypeStruct((256, 512), BF),
        in_specs=[pl.BlockSpec(memory_space=pl.ANY)] * 4,
        out_specs=pl.BlockSpec(memory_space=pltpu.VMEM),
        scratch_shapes=[
            vm(256, 512), vm(512, 1536), vm(512, 512), vm(256, 512),
            vm(256, 256), vm(256, 256), vm(512, 512),
            vm(4, 256, 128), vm(4, 256, 128), vm(1024, 128), vm(1024, 128), vm(128, 1024),
            vm(1024, 128, dtype=F32), vm(1024, 128), vm(1024, 128),
            vm(4, 256, 128), vm(4, 256, 128),
            vm(256, 512), vm(256, 256), vm(2, 256, 128), vm(2, 256, 128), vm(2, 256, 128),
            vm(2, 256, 128),
            vm(2, 256, 128, dtype=F32), vm(2, 256, 128, dtype=F32), vm(2, 256, 128, dtype=F32),
            vm(256, 512), vm(256, 512),
            pltpu.SemaphoreType.DMA((4,)), pltpu.SemaphoreType.DMA((4,)),
        ] + [pltpu.SemaphoreType.DMA((GROUP,))] * 14,
        compiler_params=pltpu.CompilerParams(
            collective_id=0, has_side_effects=True, vmem_limit_bytes=48 * 2**20
        ),
        name="axial_grads",
    )(fields.reshape(256, 512), in_weight, out_weight, cotangent.reshape(256, 512))
    return out.reshape(shape)


def solution(mesh):
    placed = (P("lon", "lat", None), P(), P(), P("lon", "lat", None))
    return jax.shard_map(
        per_device, mesh=mesh, in_specs=placed, out_specs=P("lon", "lat", None), check_vma=False
    )
```

```python
import math

import jax
import jax.numpy as jnp
from jax import lax
from jax.experimental import pallas as pl
from jax.experimental.pallas import tpu as pltpu
from jax.sharding import PartitionSpec as P

MESH = pl.DeviceIdType.MESH
BF = jnp.bfloat16
F32 = jnp.float32
NT = (((1,), (1,)), ((), ()))
NN = (((1,), (0,)), ((), ()))
TEMPER = 0.125
EXP_SCALE = TEMPER * math.log2(math.e)
GROUP = 16


def dot(a, b, dims=NN):
    return lax.dot_general(a, b, dims, preferred_element_type=F32)


def kernel(
    x_hbm, w_hbm, wo_hbm, c_hbm, out_ref,
    x, w, wo, cot, gcol, perm, wkv, mask,
    skv, sqg, rkv, rqg, kt, dkv, sendkv, sendq, retkv, retq, ss, gs,
    cx, cg, cpart, cret, css, cgs,
    in_sem, send_sem, recv_sem,
):
    lon = lax.axis_index("lon")
    lat = lax.axis_index("lat")
    my_l = lax.div(lon, 4)
    my_h = lax.rem(lon, 4)

    loads = [
        pltpu.make_async_copy(src, dst, in_sem.at[i])
        for i, (src, dst) in enumerate(((x_hbm, x), (c_hbm, cot), (wo_hbm, wo), (w_hbm, w)))
    ]
    for load in loads:
        load.start()

    x_hi, z = lax.div(lat, 8), lax.rem(lat, 8)
    lat_peers = [
        (x_hi if dx == 0 else 1 - x_hi) * 8 + lax.rem(z + dz, 8)
        for dz in (4, 3, 5, 2, 6, 1, 7, 0)
        for dx in (1, 0)
        if (dz, dx) != (0, 0)
    ]
    y, x_lo, core = lax.div(lon, 4), lax.rem(lax.div(lon, 2), 2), lax.rem(lon, 2)
    lon_peers = [
        lax.rem(y + dy, 4) * 4
        + (x_lo if dx == 0 else 1 - x_lo) * 2
        + (core if dc == 0 else 1 - core)
        for dy in (2, 1, 3, 0)
        for dx in (1, 0)
        for dc in (1, 0)
        if (dy, dx, dc) != (0, 0, 0)
    ]

    barrier = pltpu.get_barrier_semaphore()
    for p in lat_peers:
        pl.semaphore_signal(barrier, inc=1, device_id=(lon, p), device_id_type=MESH)
    for p in lon_peers:
        pl.semaphore_signal(barrier, inc=1, device_id=(p, lat), device_id_type=MESH)

    def task(ref, p, rows):
        return ref.at[lax.rem(p, 4), pl.ds(pl.multiple_of(lax.div(p, 4) * rows, rows), rows)]

    def block(ref, p, rows):
        return ref.at[pl.ds(pl.multiple_of(p * rows, rows), rows)]

    def exchange(i, peers, device, me, src, dst):
        for p in peers:
            pltpu.make_async_remote_copy(
                src_ref=src(p),
                dst_ref=dst(me),
                send_sem=send_sem.at[i],
                recv_sem=recv_sem.at[i],
                device_id=device(p),
                device_id_type=MESH,
            ).start()
        pltpu.make_async_copy(src(me), dst(me), recv_sem.at[i]).start()

    def over_lat(i, src, dst, rows):
        exchange(
            i, lat_peers, lambda p: (lon, p), lat,
            lambda p: block(src, p, rows), lambda p: block(dst, p, rows),
        )

    def to_tasks(i, src, dst):
        exchange(
            i, lon_peers, lambda p: (p, lat), lon,
            lambda p: task(src, p, 64), lambda p: block(dst, p, 64),
        )

    def from_tasks(i, src, dst, rows):
        for p in lon_peers:
            pltpu.make_async_remote_copy(
                src_ref=block(src, p, rows),
                dst_ref=task(dst, lon, rows),
                send_sem=send_sem.at[i],
                recv_sem=recv_sem.at[i],
                device_id=(p, lat),
                device_id_type=MESH,
            ).start()
        pltpu.make_async_copy(block(src, lon, rows), task(dst, lon, rows), recv_sem.at[i]).start()

    def arrived(i, ref):
        pltpu.make_async_copy(ref, ref, recv_sem.at[i]).wait()

    def sent(i, ref):
        pltpu.make_async_copy(ref, ref, send_sem.at[i]).wait()

    row = lax.broadcasted_iota(jnp.int32, (256, 256), 0)
    col = lax.broadcasted_iota(jnp.int32, (256, 256), 1)
    tile, inner = row // 64, row % 64

    def onehot(at):
        return jnp.where(col == at, 1.0, 0.0).astype(BF)

    perm[0] = onehot((inner // 4) * 16 + tile * 4 + inner % 4)
    perm[1] = onehot((inner % 16) * 16 + tile * 4 + inner // 16)
    perm[2] = onehot((row % 64) * 4 + row // 64)
    mask[...] = jnp.where((row // 4) % 4 == (col // 4) % 4, 0.0, -1e30)

    def regroup(ref, which):
        raw = jnp.concatenate([ref[b * 256 : b * 256 + 256, :] for b in range(4)], axis=1)
        return dot(perm[which], raw).astype(BF)

    def natural(ref):
        moved = regroup(ref, 0)
        return jnp.concatenate(
            [
                jnp.concatenate([moved[t * 64 : t * 64 + 64, b * 128 : b * 128 + 128] for t in range(4)], axis=1)
                for b in range(4)
            ],
            axis=0,
        )

    def lat_major(ref):
        moved = regroup(ref, 1)
        return jnp.concatenate(
            [
                jnp.concatenate(
                    [
                        moved[t * 64 + la * 16 : t * 64 + la * 16 + 16, b * 128 : b * 128 + 128]
                        for t in range(4)
                    ],
                    axis=1,
                )
                for la in range(4)
                for b in range(4)
            ],
            axis=0,
        )

    loads[0].wait()
    pl.semaphore_wait(barrier, 2 * (GROUP - 1))

    over_lat(0, x, cx, 64)
    loads[1].wait()
    loads[2].wait()
    g = dot(natural(cot), wo[...], NT).astype(BF)
    gcol[...] = g[:, 256:]
    over_lat(1, gcol, cg, 16)

    xp = lat_major(x)
    loads[3].wait()
    for h in range(4):
        wkv[:, h * 128 : h * 128 + 64] = w[:, 512 + h * 64 : 576 + h * 64]
        wkv[:, h * 128 + 64 : h * 128 + 128] = w[:, 1024 + h * 64 : 1088 + h * 64]
    kv = dot(xp, wkv[...]).astype(BF)
    for h in range(4):
        skv[h] = kv[:, h * 128 : h * 128 + 128]
    to_tasks(2, skv, rkv)
    g_row = dot(perm[2], g[:, :256])
    q = dot(xp, w[:, :256])
    for h in range(4):
        sqg[h] = jnp.concatenate(
            [q[:, h * 64 : h * 64 + 64], g_row[:, h * 64 : h * 64 + 64]], axis=1
        ).astype(BF)
    to_tasks(3, sqg, rqg)

    def fold(a, op):
        out = a[:8]
        for r in range(8, a.shape[0], 8):
            out = op(out, a[r : r + 8])
        return out

    def attend(tiles, key, value, qz, gz, s_ref, g_ref, bias, emit):
        peak = None
        for t in range(tiles):
            s = dot(key(t), qz, NT)
            if bias is not None:
                s = s + bias(t)
            s_ref[t] = s
            top = fold(s, jnp.maximum)
            peak = top if peak is None else jnp.maximum(peak, top)
        peak = jnp.max(peak, axis=0, keepdims=True) * EXP_SCALE
        total = inner_sum = jnp.zeros((8, 256), F32)
        for t in range(tiles):
            p = jnp.exp2(s_ref[t] * EXP_SCALE - peak)
            gp = dot(value(t), gz, NT)
            s_ref[t] = p
            g_ref[t] = gp
            total = total + fold(p, jnp.add)
            inner_sum = inner_sum + fold(p * gp, jnp.add)
        inv = 1.0 / jnp.sum(total, axis=0, keepdims=True)
        delta = jnp.sum(inner_sum, axis=0, keepdims=True) * inv
        for t in range(tiles):
            weights = s_ref[t] * inv
            ds = (weights * (g_ref[t] - delta)).astype(BF)
            emit(t, ds, weights.astype(BF))

    lane = lax.broadcasted_iota(jnp.int32, (256, 128), 1)
    low = lane < 64
    arrived(0, cx)
    cxv = natural(cx)
    cq = dot(cxv, w[:, 256:512])
    ck32 = dot(cxv, w[:, 768:1024]).astype(BF).astype(F32)
    cv = dot(cxv, w[:, 1280:1536]).astype(BF)
    ckt = ck32.T.astype(BF)
    ck = ck32.astype(BF)
    cq = cq.astype(BF).astype(F32)
    arrived(1, cg)
    dqt, dks, dvs = [], [], []
    for h in range(4):
        lanes = slice(h // 2 * 128, h // 2 * 128 + 128)
        mine = low if h % 2 == 0 else jnp.logical_not(low)
        qz = jnp.where(mine, cq[:, lanes], 0.0).astype(BF)
        gz = jnp.where(mine, cg[:, lanes].astype(F32), 0.0).astype(BF)
        acc = {"q": 0.0}
        dk, dv = [], []

        def emit(t, ds, wb, h=h, qz=qz, gz=gz, acc=acc, dk=dk, dv=dv):
            dk.append(dot(ds, qz))
            dv.append(dot(wb, gz))
            acc["q"] += dot(ckt[h * 64 : h * 64 + 64, t * 128 : t * 128 + 128], ds)

        attend(
            2,
            lambda t: ck[t * 128 : t * 128 + 128, lanes],
            lambda t: cv[t * 128 : t * 128 + 128, lanes],
            qz, gz, css.at[h], cgs.at[h],
            lambda t: mask[t * 128 : t * 128 + 128, :],
            emit,
        )
        dqt.append(acc["q"])
        dks.append(jnp.concatenate(dk, axis=0))
        dvs.append(jnp.concatenate(dv, axis=0))
    dq = (jnp.concatenate(dqt, axis=0).T * TEMPER).astype(BF)
    dk = (jnp.concatenate([dks[0] + dks[1], dks[2] + dks[3]], axis=1) * TEMPER).astype(BF)
    dv = jnp.concatenate([dvs[0] + dvs[1], dvs[2] + dvs[3]], axis=1).astype(BF)
    part = dot(dq, w[:, 256:512], NT) + dot(dk, w[:, 768:1024], NT) + dot(dv, w[:, 1280:1536], NT)
    cpart[...] = part.astype(BF)
    over_lat(4, cpart, cret, 16)

    arrived(2, rkv)
    kt[...] = rkv[...].astype(F32).T[:64].astype(BF)
    dkv[...] = jnp.zeros_like(dkv)
    arrived(3, rqg)

    @pl.loop(0, 4)
    def _(c):
        qg = rqg[pl.ds(pl.multiple_of(c * 256, 256), 256), :].astype(F32)
        qz = jnp.where(low, qg, 0.0).astype(BF)
        gz = jnp.where(low, 0.0, qg).astype(BF)
        acc = {"q": 0.0}

        def keys(t):
            return rkv[t * 128 : t * 128 + 128, :]

        def emit(t, ds, wb):
            dkv[t * 128 : t * 128 + 128, :] += dot(ds, qz) + dot(wb, gz)
            acc["q"] += dot(kt[:, t * 128 : t * 128 + 128], ds)

        attend(8, keys, keys, qz, gz, ss, gs, None, emit)
        dq = (acc["q"].T * TEMPER).astype(F32)
        packed = [
            jnp.concatenate([dq[i * 64 : i * 64 + 32], dq[i * 64 + 32 : i * 64 + 64]], axis=1)
            for i in range(4)
        ]
        sendq[pl.ds(pl.multiple_of(c * 128, 128), 128), :] = jnp.concatenate(packed, axis=0).astype(BF)

    from_tasks(5, sendq, retq, 32)
    lane_all = lax.broadcasted_iota(jnp.int32, (1024, 128), 1)
    sendkv[...] = (dkv[...] * jnp.where(lane_all < 64, TEMPER, 1.0)).astype(BF)
    from_tasks(6, sendkv, retkv, 64)

    arrived(5, retq)
    halves = [
        jnp.concatenate([retq[h][:, k * 64 : k * 64 + 64] for h in range(4)], axis=1)
        for k in range(2)
    ]
    dq = jnp.concatenate(
        [halves[k][la * 32 : la * 32 + 32] for la in range(4) for k in range(2)], axis=0
    )
    rp = dot(dq, w[:, :256], NT)
    arrived(6, retkv)
    rp += dot(jnp.concatenate([retkv[h] for h in range(4)], axis=1), wkv[...], NT)
    home = lax.dot_general(
        perm[2], rp.astype(BF), (((0,), (0,)), ((), ())), preferred_element_type=F32
    )
    arrived(4, cret)
    out_ref[...] = (home + cret[...].astype(F32)).astype(BF)

    sent(0, cx.at[pl.ds(0, 960)])
    sent(1, cg.at[pl.ds(0, 240)])
    sent(2, rkv.at[pl.ds(0, 960)])
    sent(3, rqg.at[pl.ds(0, 960)])
    sent(4, cret.at[pl.ds(0, 240)])
    sent(5, sendq.at[pl.ds(0, 480)])
    sent(6, sendkv.at[pl.ds(0, 960)])


def rows_of_tiles(a):
    return a.reshape(64, 4, 4, 128).transpose(0, 2, 1, 3).reshape(1024, 128)


def per_device(fields, in_weight, out_weight, cotangent):
    shape = fields.shape

    def vm(*dims, dtype=BF):
        return pltpu.VMEM(dims, dtype)

    out = pl.pallas_call(
        kernel,
        out_shape=jax.ShapeDtypeStruct((256, 512), BF),
        in_specs=[pl.BlockSpec(memory_space=pl.ANY)] * 4,
        out_specs=pl.BlockSpec(memory_space=pltpu.VMEM),
        scratch_shapes=[
            vm(1024, 128), vm(512, 1536), vm(512, 512), vm(1024, 128),
            vm(256, 256), vm(3, 256, 256), vm(512, 512), vm(256, 256, dtype=F32),
            vm(4, 256, 128), vm(4, 256, 128), vm(1024, 128), vm(1024, 128), vm(64, 1024),
            vm(1024, 128, dtype=F32), vm(1024, 128), vm(512, 128),
            vm(4, 256, 128), vm(4, 128, 128),
            vm(8, 128, 256, dtype=F32), vm(8, 128, 256, dtype=F32),
            vm(1024, 128), vm(256, 256), vm(256, 512), vm(256, 512),
            vm(4, 2, 128, 256, dtype=F32), vm(4, 2, 128, 256, dtype=F32),
            pltpu.SemaphoreType.DMA((4,)),
            pltpu.SemaphoreType.DMA((7,)), pltpu.SemaphoreType.DMA((7,)),
        ],
        compiler_params=pltpu.CompilerParams(
            collective_id=0, has_side_effects=True, vmem_limit_bytes=60 * 2**20
        ),
        name="axial_grads",
    )(rows_of_tiles(fields), in_weight, out_weight, rows_of_tiles(cotangent))
    return out.reshape(shape)


def solution(mesh):
    placed = (P("lon", "lat", None), P(), P(), P("lon", "lat", None))
    return jax.shard_map(
        per_device, mesh=mesh, in_specs=placed, out_specs=P("lon", "lat", None), check_vma=False
    )
```

```python
import math

import jax
import jax.numpy as jnp
from jax import lax
from jax.experimental import pallas as pl
from jax.experimental.pallas import tpu as pltpu
from jax.sharding import PartitionSpec as P

MESH = pl.DeviceIdType.MESH
BF = jnp.bfloat16
F32 = jnp.float32
NT = (((1,), (1,)), ((), ()))
NN = (((1,), (0,)), ((), ()))
TEMPER = 0.125
EXP_SCALE = TEMPER * math.log2(math.e)
GROUP = 16


def dot(a, b, dims=NN):
    return lax.dot_general(a, b, dims, preferred_element_type=F32)


def kernel(
    x_hbm, w_hbm, wo_hbm, c_hbm, out_ref,
    x, w, wo, cot, gcol, perm, wkv, mask,
    skv, sqg, rkv, rqg, kt, qgz, sendkv, sendq, retkv, retq, ss, gs,
    cx, cg, cpart, cret, css, cgs,
    in_sem, send_sem, recv_sem,
):
    lon = lax.axis_index("lon")
    lat = lax.axis_index("lat")
    my_l = lax.div(lon, 4)
    my_h = lax.rem(lon, 4)

    loads = [
        pltpu.make_async_copy(src, dst, in_sem.at[i])
        for i, (src, dst) in enumerate(((x_hbm, x), (c_hbm, cot), (wo_hbm, wo), (w_hbm, w)))
    ]
    for load in loads:
        load.start()

    x_hi, z = lax.div(lat, 8), lax.rem(lat, 8)
    lat_peers = [
        (x_hi if dx == 0 else 1 - x_hi) * 8 + lax.rem(z + dz, 8)
        for dz in (4, 3, 5, 2, 6, 1, 7, 0)
        for dx in (1, 0)
        if (dz, dx) != (0, 0)
    ]
    y, x_lo, core = lax.div(lon, 4), lax.rem(lax.div(lon, 2), 2), lax.rem(lon, 2)
    lon_peers = [
        lax.rem(y + dy, 4) * 4
        + (x_lo if dx == 0 else 1 - x_lo) * 2
        + (core if dc == 0 else 1 - core)
        for dy in (2, 1, 3, 0)
        for dx in (1, 0)
        for dc in (1, 0)
        if (dy, dx, dc) != (0, 0, 0)
    ]

    barrier = pltpu.get_barrier_semaphore()
    for p in lat_peers:
        pl.semaphore_signal(barrier, inc=1, device_id=(lon, p), device_id_type=MESH)
    for p in lon_peers:
        pl.semaphore_signal(barrier, inc=1, device_id=(p, lat), device_id_type=MESH)

    def task(ref, p, rows):
        return ref.at[lax.rem(p, 4), pl.ds(pl.multiple_of(lax.div(p, 4) * rows, rows), rows)]

    def block(ref, p, rows):
        return ref.at[pl.ds(pl.multiple_of(p * rows, rows), rows)]

    def exchange(i, peers, device, me, src, dst):
        for p in peers:
            pltpu.make_async_remote_copy(
                src_ref=src(p),
                dst_ref=dst(me),
                send_sem=send_sem.at[i],
                recv_sem=recv_sem.at[i],
                device_id=device(p),
                device_id_type=MESH,
            ).start()
        pltpu.make_async_copy(src(me), dst(me), recv_sem.at[i]).start()

    def over_lat(i, src, dst, rows):
        exchange(
            i, lat_peers, lambda p: (lon, p), lat,
            lambda p: block(src, p, rows), lambda p: block(dst, p, rows),
        )

    def to_tasks(i, src, dst):
        exchange(
            i, lon_peers, lambda p: (p, lat), lon,
            lambda p: task(src, p, 64), lambda p: block(dst, p, 64),
        )

    def from_tasks(i, src, dst, rows, peers):
        for p in peers:
            pltpu.make_async_remote_copy(
                src_ref=block(src, p, rows),
                dst_ref=task(dst, lon, rows),
                send_sem=send_sem.at[i],
                recv_sem=recv_sem.at[i],
                device_id=(p, lat),
                device_id_type=MESH,
            ).start()

    def arrived(i, ref):
        pltpu.make_async_copy(ref, ref, recv_sem.at[i]).wait()

    def sent(i, ref):
        pltpu.make_async_copy(ref, ref, send_sem.at[i]).wait()

    row = lax.broadcasted_iota(jnp.int32, (256, 256), 0)
    col = lax.broadcasted_iota(jnp.int32, (256, 256), 1)
    tile, inner = row // 64, row % 64

    def onehot(at):
        return jnp.where(col == at, 1.0, 0.0).astype(BF)

    perm[0] = onehot((inner // 4) * 16 + tile * 4 + inner % 4)
    perm[1] = onehot((inner % 16) * 16 + tile * 4 + inner // 16)
    perm[2] = onehot((row % 64) * 4 + row // 64)
    mask[...] = jnp.where((row // 4) % 4 == (col // 4) % 4, 0.0, -1e30)

    def regroup(ref, which):
        raw = jnp.concatenate([ref[b * 256 : b * 256 + 256, :] for b in range(4)], axis=1)
        return dot(perm[which], raw).astype(BF)

    def natural(ref):
        moved = regroup(ref, 0)
        return jnp.concatenate(
            [
                jnp.concatenate([moved[t * 64 : t * 64 + 64, b * 128 : b * 128 + 128] for t in range(4)], axis=1)
                for b in range(4)
            ],
            axis=0,
        )

    def lat_major(ref):
        moved = regroup(ref, 1)
        return jnp.concatenate(
            [
                jnp.concatenate(
                    [
                        moved[t * 64 + la * 16 : t * 64 + la * 16 + 16, b * 128 : b * 128 + 128]
                        for t in range(4)
                    ],
                    axis=1,
                )
                for la in range(4)
                for b in range(4)
            ],
            axis=0,
        )

    loads[0].wait()
    pl.semaphore_wait(barrier, 2 * (GROUP - 1))

    over_lat(0, x, cx, 64)
    loads[1].wait()
    loads[2].wait()
    g = dot(natural(cot), wo[...], NT).astype(BF)
    gcol[...] = g[:, 256:]
    over_lat(1, gcol, cg, 16)

    xp = lat_major(x)
    loads[3].wait()
    for h in range(4):
        wkv[:, h * 128 : h * 128 + 64] = w[:, 512 + h * 64 : 576 + h * 64]
        wkv[:, h * 128 + 64 : h * 128 + 128] = w[:, 1024 + h * 64 : 1088 + h * 64]
    kv = dot(xp, wkv[...]).astype(BF)
    for h in range(4):
        skv[h] = kv[:, h * 128 : h * 128 + 128]
    to_tasks(2, skv, rkv)
    g_row = dot(perm[2], g[:, :256])
    q = dot(xp, w[:, :256])
    for h in range(4):
        sqg[h] = jnp.concatenate(
            [q[:, h * 64 : h * 64 + 64], g_row[:, h * 64 : h * 64 + 64]], axis=1
        ).astype(BF)
    to_tasks(3, sqg, rqg)

    def fold(a, op):
        out = a[:8]
        for r in range(8, a.shape[0], 8):
            out = op(out, a[r : r + 8])
        return out

    def softmax_stats(tiles, key, value, qz, gz, s_ref, g_ref, bias):
        size = s_ref.shape[0] // tiles
        peak = None
        for t in range(tiles):
            s = dot(key(t), qz, NT)
            if bias is not None:
                s = s + bias(t)
            s_ref[t * size : t * size + size] = s
            top = fold(s, jnp.maximum)
            peak = top if peak is None else jnp.maximum(peak, top)
        peak = jnp.max(peak, axis=0, keepdims=True) * EXP_SCALE
        total = inner_sum = jnp.zeros((8, 256), F32)
        for t in range(tiles):
            at = slice(t * size, t * size + size)
            p = jnp.exp2(s_ref[at] * EXP_SCALE - peak)
            gp = dot(value(t), gz, NT)
            s_ref[at] = p
            g_ref[at] = gp
            total = total + fold(p, jnp.add)
            inner_sum = inner_sum + fold(p * gp, jnp.add)
        inv = 1.0 / jnp.sum(total, axis=0, keepdims=True)
        return inv, jnp.sum(inner_sum, axis=0, keepdims=True) * inv

    lane = lax.broadcasted_iota(jnp.int32, (256, 128), 1)
    low = lane < 64
    arrived(0, cx)
    cxv = natural(cx)
    cq = dot(cxv, w[:, 256:512])
    ck32 = dot(cxv, w[:, 768:1024]).astype(BF).astype(F32)
    cv = dot(cxv, w[:, 1280:1536]).astype(BF)
    ckt = ck32.T.astype(BF)
    ck = ck32.astype(BF)
    cq = cq.astype(BF).astype(F32)
    arrived(1, cg)
    dqt, dks, dvs = [], [], []
    for h in range(4):
        lanes = slice(h // 2 * 128, h // 2 * 128 + 128)
        mine = low if h % 2 == 0 else jnp.logical_not(low)
        qz = jnp.where(mine, cq[:, lanes], 0.0).astype(BF)
        gz = jnp.where(mine, cg[:, lanes].astype(F32), 0.0).astype(BF)
        inv, delta = softmax_stats(
            2,
            lambda t: ck[t * 128 : t * 128 + 128, lanes],
            lambda t: cv[t * 128 : t * 128 + 128, lanes],
            qz, gz, css.at[h], cgs.at[h],
            lambda t: mask[t * 128 : t * 128 + 128, :],
        )
        weights = css[h] * inv
        ds = (weights * (cgs[h] - delta)).astype(BF)
        dks.append(dot(ds, qz))
        dvs.append(dot(weights.astype(BF), gz))
        dqt.append(dot(ckt[h * 64 : h * 64 + 64], ds))
    dq = (jnp.concatenate(dqt, axis=0).T * TEMPER).astype(BF)
    dk = (jnp.concatenate([dks[0] + dks[1], dks[2] + dks[3]], axis=1) * TEMPER).astype(BF)
    dv = jnp.concatenate([dvs[0] + dvs[1], dvs[2] + dvs[3]], axis=1).astype(BF)
    part = dot(dq, w[:, 256:512], NT) + dot(dk, w[:, 768:1024], NT) + dot(dv, w[:, 1280:1536], NT)
    cpart[...] = part.astype(BF)
    over_lat(4, cpart, cret, 16)

    arrived(2, rkv)
    keys_t = rkv[...].astype(F32).T[:64].astype(BF)
    for t in range(4):
        kt[t] = keys_t[:, t * 256 : t * 256 + 256]
    arrived(3, rqg)
    stats = []
    for c in range(4):
        qg = rqg[c * 256 : c * 256 + 256, :].astype(F32)
        qgz[c, :256] = jnp.where(low, qg, 0.0).astype(BF)
        qgz[c, 256:] = jnp.where(low, 0.0, qg).astype(BF)

        def keys(t):
            return rkv[t * 128 : t * 128 + 128, :]

        stats.append(
            softmax_stats(8, keys, keys, qgz[c, :256], qgz[c, 256:], ss.at[c], gs.at[c], None)
        )

    dqt = [jnp.zeros((64, 256), F32) for _ in range(4)]
    half_scale = jnp.where(low, TEMPER, 1.0)
    for dy in (2, 1, 3, 0):
        at = lax.rem(y + dy, 4)
        rows = pl.ds(pl.multiple_of(at * 256, 256), 256)
        acc = jnp.zeros((256, 128), F32)
        for c in range(4):
            inv, delta = stats[c]
            weights = ss[c, rows] * inv
            ds = (weights * (gs[c, rows] - delta)).astype(BF)
            acc += dot(ds, qgz[c, :256]) + dot(weights.astype(BF), qgz[c, 256:])
            dqt[c] += dot(kt[at], ds)
        sendkv[rows, :] = (acc * half_scale).astype(BF)
        from_tasks(6, sendkv, retkv, 64, lon_peers[4 * ((2, 1, 3, 0).index(dy)) :][:4])
    pltpu.make_async_copy(block(sendkv, lon, 64), task(retkv, lon, 64), recv_sem.at[6]).start()
    for c in range(4):
        dq = dqt[c].T * TEMPER
        packed = [
            jnp.concatenate([dq[i * 64 : i * 64 + 32], dq[i * 64 + 32 : i * 64 + 64]], axis=1)
            for i in range(4)
        ]
        sendq[c * 128 : c * 128 + 128, :] = jnp.concatenate(packed, axis=0).astype(BF)
    from_tasks(5, sendq, retq, 32, lon_peers)
    pltpu.make_async_copy(block(sendq, lon, 32), task(retq, lon, 32), recv_sem.at[5]).start()

    arrived(6, retkv)
    rp = dot(jnp.concatenate([retkv[h] for h in range(4)], axis=1), wkv[...], NT)
    arrived(5, retq)
    halves = [
        jnp.concatenate([retq[h][:, k * 64 : k * 64 + 64] for h in range(4)], axis=1)
        for k in range(2)
    ]
    dq = jnp.concatenate(
        [halves[k][la * 32 : la * 32 + 32] for la in range(4) for k in range(2)], axis=0
    )
    rp += dot(dq, w[:, :256], NT)
    home = lax.dot_general(
        perm[2], rp.astype(BF), (((0,), (0,)), ((), ())), preferred_element_type=F32
    )
    arrived(4, cret)
    out_ref[...] = (home + cret[...].astype(F32)).astype(BF)

    sent(0, cx.at[pl.ds(0, 960)])
    sent(1, cg.at[pl.ds(0, 240)])
    sent(2, rkv.at[pl.ds(0, 960)])
    sent(3, rqg.at[pl.ds(0, 960)])
    sent(4, cret.at[pl.ds(0, 240)])
    sent(5, sendq.at[pl.ds(0, 480)])
    sent(6, sendkv.at[pl.ds(0, 960)])


def rows_of_tiles(a):
    return a.reshape(64, 4, 4, 128).transpose(0, 2, 1, 3).reshape(1024, 128)


def per_device(fields, in_weight, out_weight, cotangent):
    shape = fields.shape

    def vm(*dims, dtype=BF):
        return pltpu.VMEM(dims, dtype)

    out = pl.pallas_call(
        kernel,
        out_shape=jax.ShapeDtypeStruct((256, 512), BF),
        in_specs=[pl.BlockSpec(memory_space=pl.ANY)] * 4,
        out_specs=pl.BlockSpec(memory_space=pltpu.VMEM),
        scratch_shapes=[
            vm(1024, 128), vm(512, 1536), vm(512, 512), vm(1024, 128),
            vm(256, 256), vm(3, 256, 256), vm(512, 512), vm(256, 256, dtype=F32),
            vm(4, 256, 128), vm(4, 256, 128), vm(1024, 128), vm(1024, 128), vm(4, 64, 256),
            vm(4, 512, 128), vm(1024, 128), vm(512, 128),
            vm(4, 256, 128), vm(4, 128, 128),
            vm(4, 1024, 256, dtype=F32), vm(4, 1024, 256, dtype=F32),
            vm(1024, 128), vm(256, 256), vm(256, 512), vm(256, 512),
            vm(4, 256, 256, dtype=F32), vm(4, 256, 256, dtype=F32),
            pltpu.SemaphoreType.DMA((4,)),
            pltpu.SemaphoreType.DMA((7,)), pltpu.SemaphoreType.DMA((7,)),
        ],
        compiler_params=pltpu.CompilerParams(
            collective_id=0, has_side_effects=True, vmem_limit_bytes=40 * 2**20
        ),
        name="axial_grads",
    )(*(
        pltpu.with_memory_space_constraint(a, pltpu.HBM)
        for a in (rows_of_tiles(fields), in_weight, out_weight, rows_of_tiles(cotangent))
    ))
    return out.reshape(shape)


def solution(mesh):
    placed = (P("lon", "lat", None), P(), P(), P("lon", "lat", None))
    return jax.shard_map(
        per_device, mesh=mesh, in_specs=placed, out_specs=P("lon", "lat", None), check_vma=False
    )
```

```python
import math

import jax
import jax.numpy as jnp
from jax import lax
from jax.experimental import pallas as pl
from jax.experimental.pallas import tpu as pltpu
from jax.sharding import PartitionSpec as P

MESH = pl.DeviceIdType.MESH
BF = jnp.bfloat16
F32 = jnp.float32
NT = (((1,), (1,)), ((), ()))
NN = (((1,), (0,)), ((), ()))
TEMPER = 0.125
EXP_SCALE = TEMPER * math.log2(math.e)
GROUP = 16


def dot(a, b, dims=NN):
    return lax.dot_general(a, b, dims, preferred_element_type=F32)


def kernel(
    x_hbm, w_hbm, wo_hbm, c_hbm, out_ref,
    x, w, wo, cot, perm, wkv, mask,
    skv, sqg, rkv, rqg, kt, qgz, sendkv, sendq, retkv, retq, ss, gs,
    xg, cxg, cpart, cret, css, cgs,
    in_sem, send_sem, recv_sem, chunk_sem,
):
    lon = lax.axis_index("lon")
    lat = lax.axis_index("lat")
    my_l = lax.div(lon, 4)
    my_h = lax.rem(lon, 4)

    loads = [
        pltpu.make_async_copy(src, dst, in_sem.at[i])
        for i, (src, dst) in enumerate(((x_hbm, x), (c_hbm, cot), (wo_hbm, wo), (w_hbm, w)))
    ]
    for load in loads:
        load.start()

    z_lat = lax.rem(lat, 8)
    lat_peers = [
        x_hi * 8 + lax.rem(z_lat + dz, 8) for dz in (4, 3, 5, 2, 6, 1, 7, 0) for x_hi in (0, 1)
    ]
    y, x_lo, core = lax.div(lon, 4), lax.rem(lax.div(lon, 2), 2), lax.rem(lon, 2)
    beside = y * 4 + (1 - x_lo) * 2 + core
    lon_peers = [
        lax.rem(y + dy, 4) * 4
        + (x_lo if dx == 0 else 1 - x_lo) * 2
        + (core if dc == 0 else 1 - core)
        for dy in (2, 1, 3, 0)
        for dx in (1, 0)
        for dc in (1, 0)
        if (dy, dx, dc) != (0, 0, 0)
    ]

    barrier = pltpu.get_barrier_semaphore()
    for p in lat_peers:
        pl.semaphore_signal(barrier, inc=1, device_id=(beside, p), device_id_type=MESH)
    for p in lon_peers:
        pl.semaphore_signal(barrier, inc=1, device_id=(p, lat), device_id_type=MESH)

    def task(ref, p, rows):
        return ref.at[lax.rem(p, 4), pl.ds(pl.multiple_of(lax.div(p, 4) * rows, rows), rows)]

    def block(ref, p, rows):
        return ref.at[pl.ds(pl.multiple_of(p * rows, rows), rows)]

    def over_lat(i, src, dst, rows):
        for p in lat_peers:
            pltpu.make_async_remote_copy(
                src_ref=block(src, p, rows),
                dst_ref=block(dst, lat, rows),
                send_sem=send_sem.at[i],
                recv_sem=recv_sem.at[i],
                device_id=(beside, p),
                device_id_type=MESH,
            ).start()

    def to_tasks(i, src, dst, landed):
        for p in lon_peers:
            pltpu.make_async_remote_copy(
                src_ref=task(src, p, 64),
                dst_ref=block(dst, lon, 64),
                send_sem=send_sem.at[i],
                recv_sem=landed,
                device_id=(p, lat),
                device_id_type=MESH,
            ).start()
        pltpu.make_async_copy(task(src, lon, 64), block(dst, lon, 64), landed).start()

    def from_tasks(i, src, dst, rows, peers):
        for p in peers:
            pltpu.make_async_remote_copy(
                src_ref=block(src, p, rows),
                dst_ref=task(dst, lon, rows),
                send_sem=send_sem.at[i],
                recv_sem=recv_sem.at[i],
                device_id=(p, lat),
                device_id_type=MESH,
            ).start()

    def arrived(i, ref):
        pltpu.make_async_copy(ref, ref, recv_sem.at[i]).wait()

    def sent(i, ref):
        pltpu.make_async_copy(ref, ref, send_sem.at[i]).wait()

    row = lax.broadcasted_iota(jnp.int32, (256, 256), 0)
    col = lax.broadcasted_iota(jnp.int32, (256, 256), 1)
    tile, inner = row // 64, row % 64

    def onehot(at):
        return jnp.where(col == at, 1.0, 0.0).astype(BF)

    perm[0] = onehot((inner // 4) * 16 + tile * 4 + inner % 4)
    perm[1] = onehot((inner % 16) * 16 + tile * 4 + inner // 16)
    perm[2] = onehot((row % 64) * 4 + row // 64)
    row = lax.broadcasted_iota(jnp.int32, (128, 512), 0)
    col = lax.broadcasted_iota(jnp.int32, (128, 512), 1)
    mask[...] = jnp.where((row // 4) % 2 == (col // 4) % 2, 0.0, -1e30)

    def regroup(blocks, which):
        return dot(perm[which], jnp.concatenate(blocks, axis=1)).astype(BF)

    def natural(blocks):
        moved = regroup(blocks, 0)
        return jnp.concatenate(
            [
                jnp.concatenate(
                    [moved[t * 64 : t * 64 + 64, b * 128 : b * 128 + 128] for t in range(4)], axis=1
                )
                for b in range(len(blocks))
            ],
            axis=0,
        )

    def quarters(ref):
        return [ref[b * 256 : b * 256 + 256, :] for b in range(4)]

    def lat_major(blocks):
        moved = regroup(blocks, 1)
        return jnp.concatenate(
            [
                jnp.concatenate(
                    [
                        moved[t * 64 + la * 16 : t * 64 + la * 16 + 16, b * 128 : b * 128 + 128]
                        for t in range(4)
                    ],
                    axis=1,
                )
                for la in range(4)
                for b in range(4)
            ],
            axis=0,
        )

    loads[1].wait()
    loads[2].wait()
    g = dot(natural(quarters(cot)), wo[...], NT)
    loads[0].wait()
    for half in range(2):
        for p in range(GROUP):
            xg[half, p * 48 : p * 48 + 32, :] = x[p * 64 + half * 32 : p * 64 + half * 32 + 32, :]
            xg[half, p * 48 + 32 : p * 48 + 48, :] = jnp.concatenate(
                [
                    g[p * 16 + half * 8 : p * 16 + half * 8 + 8, 256 + t * 128 : 384 + t * 128]
                    for t in range(2)
                ],
                axis=0,
            ).astype(BF)

    def front_row():
        xp = lat_major(quarters(x))
        loads[3].wait()
        for h in range(4):
            wkv[:, h * 128 : h * 128 + 64] = w[:, 512 + h * 64 : 576 + h * 64]
            wkv[:, h * 128 + 64 : h * 128 + 128] = w[:, 1024 + h * 64 : 1088 + h * 64]
        kv = dot(xp, wkv[...]).astype(BF)
        g_row = dot(perm[2], g[:, :256].astype(BF))
        q = dot(xp, w[:, :256])
        for h in range(4):
            skv[h] = kv[:, h * 128 : h * 128 + 128]
            sqg[h] = jnp.concatenate(
                [q[:, h * 64 : h * 64 + 64], g_row[:, h * 64 : h * 64 + 64]], axis=1
            ).astype(BF)

    front_row()
    pl.semaphore_wait(barrier, 2 * GROUP - 1)
    to_tasks(2, skv, rkv, recv_sem.at[2])
    to_tasks(3, sqg, rqg, chunk_sem.at[y])
    over_lat(0, xg.at[0], cxg.at[0], 48)
    over_lat(1, xg.at[1], cxg.at[1], 48)
    def fold(a, op):
        out = a[:8]
        for r in range(8, a.shape[0], 8):
            out = op(out, a[r : r + 8])
        return out

    def softmax_stats(tiles, key, value, qz, gz, s_ref, g_ref, bias):
        size = s_ref.shape[0] // tiles
        peak = None
        for t in range(tiles):
            s = dot(key(t), qz, NT)
            if bias is not None:
                s = s + bias(t)
            s_ref[t * size : t * size + size] = s
            top = fold(s, jnp.maximum)
            peak = top if peak is None else jnp.maximum(peak, top)
        peak = jnp.max(peak, axis=0, keepdims=True) * EXP_SCALE
        total = inner_sum = jnp.zeros((8, qz.shape[0]), F32)
        for t in range(tiles):
            at = slice(t * size, t * size + size)
            p = jnp.exp2(s_ref[at] * EXP_SCALE - peak)
            gp = dot(value(t), gz, NT)
            s_ref[at] = p
            g_ref[at] = gp
            total = total + fold(p, jnp.add)
            inner_sum = inner_sum + fold(p * gp, jnp.add)
        inv = 1.0 / jnp.sum(total, axis=0, keepdims=True)
        return inv, jnp.sum(inner_sum, axis=0, keepdims=True) * inv

    low = lax.broadcasted_iota(jnp.int32, (256, 128), 1) < 64
    head_of_lane = lax.broadcasted_iota(jnp.int32, (128, 256), 1) // 64

    def columns(half, i_in, i_out):
        arrived(i_in, cxg.at[half])
        got = cxg.at[half]
        tokens = natural(
            [
                jnp.concatenate(
                    [got[p * 48 : p * 48 + 32, :] for p in range(b * 8, b * 8 + 8)], axis=0
                )
                for b in range(2)
            ]
        )
        grads = [got[p * 48 + 32 : p * 48 + 48, :].astype(F32) for p in range(GROUP)]
        grads = jnp.concatenate(
            [
                jnp.concatenate([a[t * 8 : t * 8 + 8] for a in grads], axis=0) for t in range(2)
            ],
            axis=1,
        )
        q = dot(tokens, w[:, 256:512]).astype(BF).astype(F32)
        k = dot(tokens, w[:, 768:1024]).astype(BF)
        v = dot(tokens, w[:, 1280:1536]).astype(BF)
        k_t = k.astype(F32).T.astype(BF)

        def by_head(a):
            return jnp.concatenate(
                [jnp.where(head_of_lane == h, a, 0.0).astype(BF) for h in range(4)], axis=0
            )

        qz, gz = by_head(q), by_head(grads)
        s_ref, g_ref = css.at[half], cgs.at[half]
        inv, delta = softmax_stats(
            1, lambda t: k, lambda t: v, qz, gz, s_ref, g_ref, lambda t: mask[...]
        )
        weights = s_ref[...] * inv
        ds = (weights * (g_ref[...] - delta)).astype(BF)
        dk = (dot(ds, qz) * TEMPER).astype(BF)
        dv = dot(weights.astype(BF), gz).astype(BF)
        dq_t = jnp.concatenate(
            [dot(k_t[h * 64 : h * 64 + 64], ds[:, h * 128 : h * 128 + 128]) for h in range(4)],
            axis=0,
        )
        dq = (dq_t.T * TEMPER).astype(BF)
        part = (
            dot(dq, w[:, 256:512], NT) + dot(dk, w[:, 768:1024], NT) + dot(dv, w[:, 1280:1536], NT)
        )
        for p in range(GROUP):
            cpart[half, p * 32 : p * 32 + 32, :] = jnp.concatenate(
                [part[p * 8 : p * 8 + 8, t * 128 : t * 128 + 128] for t in range(4)], axis=0
            ).astype(BF)
        over_lat(i_out, cpart.at[half], cret.at[half], 32)

    def chunk_rows(dy, size):
        return pl.ds(pl.multiple_of(lax.rem(y + dy, 4) * size, size), size)

    def row_stats():
        arrived(2, rkv)
        keys_t = rkv[...].astype(F32).T[:64].astype(BF)
        for t in range(4):
            kt[t] = keys_t[:, t * 256 : t * 256 + 256]
        stats = []
        for c, dy in enumerate((0, 1, 3, 2)):
            rows = rqg.at[chunk_rows(dy, 256)]
            pltpu.make_async_copy(rows, rows, chunk_sem.at[lax.rem(y + dy, 4)]).wait()
            qg = rows[...].astype(F32)
            qgz[c, :256] = jnp.where(low, qg, 0.0).astype(BF)
            qgz[c, 256:] = jnp.where(low, 0.0, qg).astype(BF)

            def keys(t):
                return rkv[t * 128 : t * 128 + 128, :]

            stats.append(
                softmax_stats(8, keys, keys, qgz[c, :256], qgz[c, 256:], ss.at[c], gs.at[c], None)
            )
        return stats

    def row_grads(stats):
        dqt = [jnp.zeros((64, 256), F32) for _ in range(4)]
        half_scale = jnp.where(low, TEMPER, 1.0)
        for dy in (2, 1, 3, 0):
            at = lax.rem(y + dy, 4)
            rows = pl.ds(pl.multiple_of(at * 256, 256), 256)
            acc = jnp.zeros((256, 128), F32)
            for c in range(4):
                inv, delta = stats[c]
                weights = ss[c, rows] * inv
                ds = (weights * (gs[c, rows] - delta)).astype(BF)
                acc += dot(ds, qgz[c, :256]) + dot(weights.astype(BF), qgz[c, 256:])
                dqt[c] += dot(kt[at], ds)
            sendkv[rows, :] = (acc * half_scale).astype(BF)
            from_tasks(6, sendkv, retkv, 64, lon_peers[4 * ((2, 1, 3, 0).index(dy)) :][:4])
        pltpu.make_async_copy(block(sendkv, lon, 64), task(retkv, lon, 64), recv_sem.at[6]).start()
        for c, dy in ((3, 2), (1, 1), (2, 3), (0, 0)):
            dq = dqt[c].T * TEMPER
            packed = [
                jnp.concatenate([dq[i * 64 : i * 64 + 32], dq[i * 64 + 32 : i * 64 + 64]], axis=1)
                for i in range(4)
            ]
            sendq[chunk_rows(dy, 128), :] = jnp.concatenate(packed, axis=0).astype(BF)
            from_tasks(5, sendq, retq, 32, lon_peers[4 * ((2, 1, 3, 0).index(dy)) :][:4])
        pltpu.make_async_copy(block(sendq, lon, 32), task(retq, lon, 32), recv_sem.at[5]).start()

    columns(0, 0, 4)
    stats = row_stats()
    row_grads(stats)
    columns(1, 1, 7)

    def home(a):
        return lax.dot_general(
            perm[2], a, (((0,), (0,)), ((), ())), preferred_element_type=F32
        ).astype(BF)

    arrived(4, cret.at[0])
    arrived(7, cret.at[1])
    back = [cret[half].astype(F32) for half in range(2)]
    total = jnp.concatenate(
        [
            jnp.concatenate(
                [
                    back[half][p * 32 + t * 8 : p * 32 + t * 8 + 8]
                    for p in range(GROUP)
                    for half in range(2)
                ],
                axis=0,
            )
            for t in range(4)
        ],
        axis=1,
    )
    arrived(6, retkv)
    total += dot(home(jnp.concatenate([retkv[h] for h in range(4)], axis=1)), wkv[...], NT)
    arrived(5, retq)
    halves = [
        jnp.concatenate([retq[h][:, k * 64 : k * 64 + 64] for h in range(4)], axis=1)
        for k in range(2)
    ]
    dq = jnp.concatenate(
        [halves[k][la * 32 : la * 32 + 32] for la in range(4) for k in range(2)], axis=0
    )
    out_ref[...] = (total + dot(home(dq), w[:, :256], NT)).astype(BF)

    sent(0, cxg.at[0])
    sent(1, cxg.at[1])
    sent(2, rkv.at[pl.ds(0, 960)])
    sent(3, rqg.at[pl.ds(0, 960)])
    sent(4, cret.at[0])
    sent(7, cret.at[1])
    sent(5, sendq.at[pl.ds(0, 480)])
    sent(6, sendkv.at[pl.ds(0, 960)])


def rows_of_tiles(a):
    return a.reshape(64, 4, 4, 128).transpose(0, 2, 1, 3).reshape(1024, 128)


def per_device(fields, in_weight, out_weight, cotangent):
    shape = fields.shape

    def vm(*dims, dtype=BF):
        return pltpu.VMEM(dims, dtype)

    out = pl.pallas_call(
        kernel,
        out_shape=jax.ShapeDtypeStruct((256, 512), BF),
        in_specs=[pl.BlockSpec(memory_space=pl.ANY)] * 4,
        out_specs=pl.BlockSpec(memory_space=pltpu.VMEM),
        scratch_shapes=[
            vm(1024, 128), vm(512, 1536), vm(512, 512), vm(1024, 128),
            vm(3, 256, 256), vm(512, 512), vm(128, 512, dtype=F32),
            vm(4, 256, 128), vm(4, 256, 128), vm(1024, 128), vm(1024, 128), vm(4, 64, 256),
            vm(4, 512, 128), vm(1024, 128), vm(512, 128),
            vm(4, 256, 128), vm(4, 128, 128),
            vm(4, 1024, 256, dtype=F32), vm(4, 1024, 256, dtype=F32),
            vm(2, 768, 128), vm(2, 768, 128), vm(2, 512, 128), vm(2, 512, 128),
            vm(2, 128, 512, dtype=F32), vm(2, 128, 512, dtype=F32),
            pltpu.SemaphoreType.DMA((4,)),
            pltpu.SemaphoreType.DMA((8,)), pltpu.SemaphoreType.DMA((8,)),
            pltpu.SemaphoreType.DMA((4,)),
        ],
        compiler_params=pltpu.CompilerParams(
            collective_id=0, has_side_effects=True, vmem_limit_bytes=40 * 2**20
        ),
        name="axial_grads",
    )(*(
        pltpu.with_memory_space_constraint(a, pltpu.HBM)
        for a in (rows_of_tiles(fields), in_weight, out_weight, rows_of_tiles(cotangent))
    ))
    return out.reshape(shape)


def solution(mesh):
    placed = (P("lon", "lat", None), P(), P(), P("lon", "lat", None))
    return jax.shard_map(
        per_device, mesh=mesh, in_specs=placed, out_specs=P("lon", "lat", None), check_vma=False
    )
```

```python
import math

import jax
import jax.numpy as jnp
from jax import lax
from jax.experimental import pallas as pl
from jax.experimental.pallas import tpu as pltpu
from jax.sharding import PartitionSpec as P

MESH = pl.DeviceIdType.MESH
BF = jnp.bfloat16
F32 = jnp.float32
NT = (((1,), (1,)), ((), ()))
NN = (((1,), (0,)), ((), ()))
TEMPER = 0.125
EXP_SCALE = TEMPER * math.log2(math.e)
GROUP = 16


def dot(a, b, dims=NN):
    return lax.dot_general(a, b, dims, preferred_element_type=F32)


def kernel(
    x_hbm, w_hbm, wo_hbm, c_hbm, out_ref,
    x, w, wo, cot, perm, wkv, mask,
    skv, sqg, rkv, rqg, kt, qgz, sendkv, sendq, retkv, retq, ss, gs,
    xg, cxg, cpart, cret, css, cgs,
    in_sem, send_sem, recv_sem, chunk_sem, mate_sem,
):
    lon = lax.axis_index("lon")
    lat = lax.axis_index("lat")
    my_l = lax.div(lon, 4)
    my_h = lax.rem(lon, 4)

    loads = [
        pltpu.make_async_copy(src, dst, in_sem.at[i])
        for i, (src, dst) in enumerate(((x_hbm, x), (c_hbm, cot), (wo_hbm, wo), (w_hbm, w)))
    ]
    for load in loads:
        load.start()

    z_lat = lax.rem(lat, 8)
    lat_peers = [
        x_hi * 8 + lax.rem(z_lat + dz, 8) for dz in (4, 3, 5, 2, 6, 1, 7, 0) for x_hi in (0, 1)
    ]
    y, x_lo, core = lax.div(lon, 4), lax.rem(lax.div(lon, 2), 2), lax.rem(lon, 2)
    beside = y * 4 + (1 - x_lo) * 2 + core
    lon_peers = [
        lax.rem(y + dy, 4) * 4
        + (x_lo if dx == 0 else 1 - x_lo) * 2
        + (core if dc == 0 else 1 - core)
        for dy in (2, 1, 3, 0)
        for dx in (1, 0)
        for dc in (1, 0)
        if (dy, dx, dc) != (0, 0, 0)
    ]

    barrier = pltpu.get_barrier_semaphore()
    mate = lon + 1 - 2 * core
    for p in lat_peers:
        pl.semaphore_signal(
            barrier, inc=1, device_id=(beside + 1 - core, p), device_id_type=MESH
        )
    for dy in (2, 1, 3, 0):
        for dx in (1, 0):
            chip = lax.rem(y + dy, 4) * 4 + (x_lo if dx == 0 else 1 - x_lo) * 2
            if (dy, dx) != (0, 0):
                pl.semaphore_signal(barrier, inc=1, device_id=(chip, lat), device_id_type=MESH)
            else:

                @pl.when(core == 1)
                def _():
                    pl.semaphore_signal(barrier, inc=1, device_id=(mate, lat), device_id_type=MESH)

    def lon_group_entered():
        @pl.when(core == 0)
        def _():
            pl.semaphore_wait(barrier, GROUP - 1)
            pl.semaphore_signal(mate_sem.at[0], inc=1, device_id=(mate, lat), device_id_type=MESH)

        @pl.when(core == 1)
        def _():
            pl.semaphore_wait(mate_sem.at[0], 1)

    def columns_entered():
        @pl.when(core == 1)
        def _():
            pl.semaphore_wait(barrier, 2 * GROUP)
            pl.semaphore_signal(mate_sem.at[1], inc=1, device_id=(mate, lat), device_id_type=MESH)

        @pl.when(core == 0)
        def _():
            pl.semaphore_wait(mate_sem.at[1], 1)

    def task(ref, p, rows):
        return ref.at[lax.rem(p, 4), pl.ds(pl.multiple_of(lax.div(p, 4) * rows, rows), rows)]

    def block(ref, p, rows):
        return ref.at[pl.ds(pl.multiple_of(p * rows, rows), rows)]

    def over_lat(i, src, dst, rows):
        for p in lat_peers:
            pltpu.make_async_remote_copy(
                src_ref=block(src, p, rows),
                dst_ref=block(dst, lat, rows),
                send_sem=send_sem.at[i],
                recv_sem=recv_sem.at[i],
                device_id=(beside, p),
                device_id_type=MESH,
            ).start()

    def to_tasks(i, src, dst, landed):
        for p in lon_peers:
            pltpu.make_async_remote_copy(
                src_ref=task(src, p, 64),
                dst_ref=block(dst, lon, 64),
                send_sem=send_sem.at[i],
                recv_sem=landed,
                device_id=(p, lat),
                device_id_type=MESH,
            ).start()
        pltpu.make_async_copy(task(src, lon, 64), block(dst, lon, 64), landed).start()

    def from_tasks(i, src, dst, rows, peers):
        for p in peers:
            pltpu.make_async_remote_copy(
                src_ref=block(src, p, rows),
                dst_ref=task(dst, lon, rows),
                send_sem=send_sem.at[i],
                recv_sem=recv_sem.at[i],
                device_id=(p, lat),
                device_id_type=MESH,
            ).start()

    def arrived(i, ref):
        pltpu.make_async_copy(ref, ref, recv_sem.at[i]).wait()

    def sent(i, ref):
        pltpu.make_async_copy(ref, ref, send_sem.at[i]).wait()

    row = lax.broadcasted_iota(jnp.int32, (256, 256), 0)
    col = lax.broadcasted_iota(jnp.int32, (256, 256), 1)
    tile, inner = row // 64, row % 64

    def onehot(at):
        return jnp.where(col == at, 1.0, 0.0).astype(BF)

    perm[0] = onehot((inner // 4) * 16 + tile * 4 + inner % 4)
    perm[1] = onehot((inner % 16) * 16 + tile * 4 + inner // 16)
    perm[2] = onehot((row % 64) * 4 + row // 64)
    row = lax.broadcasted_iota(jnp.int32, (128, 512), 0)
    col = lax.broadcasted_iota(jnp.int32, (128, 512), 1)
    mask[...] = jnp.where((row // 4) % 2 == (col // 4) % 2, 0.0, -1e30)

    def regroup(blocks, which):
        return dot(perm[which], jnp.concatenate(blocks, axis=1)).astype(BF)

    def natural(blocks):
        moved = regroup(blocks, 0)
        return jnp.concatenate(
            [
                jnp.concatenate(
                    [moved[t * 64 : t * 64 + 64, b * 128 : b * 128 + 128] for t in range(4)], axis=1
                )
                for b in range(len(blocks))
            ],
            axis=0,
        )

    def quarters(ref):
        return [ref[b * 256 : b * 256 + 256, :] for b in range(4)]

    def lat_major(blocks):
        moved = regroup(blocks, 1)
        return jnp.concatenate(
            [
                jnp.concatenate(
                    [
                        moved[t * 64 + la * 16 : t * 64 + la * 16 + 16, b * 128 : b * 128 + 128]
                        for t in range(4)
                    ],
                    axis=1,
                )
                for la in range(4)
                for b in range(4)
            ],
            axis=0,
        )

    loads[1].wait()
    loads[2].wait()
    g = dot(natural(quarters(cot)), wo[...], NT)
    loads[0].wait()
    for half in range(2):
        for p in range(GROUP):
            xg[half, p * 48 : p * 48 + 32, :] = x[p * 64 + half * 32 : p * 64 + half * 32 + 32, :]
            xg[half, p * 48 + 32 : p * 48 + 48, :] = jnp.concatenate(
                [
                    g[p * 16 + half * 8 : p * 16 + half * 8 + 8, 256 + t * 128 : 384 + t * 128]
                    for t in range(2)
                ],
                axis=0,
            ).astype(BF)

    def front_row():
        xp = lat_major(quarters(x))
        loads[3].wait()
        for h in range(4):
            wkv[:, h * 128 : h * 128 + 64] = w[:, 512 + h * 64 : 576 + h * 64]
            wkv[:, h * 128 + 64 : h * 128 + 128] = w[:, 1024 + h * 64 : 1088 + h * 64]
        kv = dot(xp, wkv[...]).astype(BF)
        g_row = dot(perm[2], g[:, :256].astype(BF))
        q = dot(xp, w[:, :256])
        for h in range(4):
            skv[h] = kv[:, h * 128 : h * 128 + 128]
            sqg[h] = jnp.concatenate(
                [q[:, h * 64 : h * 64 + 64], g_row[:, h * 64 : h * 64 + 64]], axis=1
            ).astype(BF)

    early = z_lat < 4

    def send_rows():
        to_tasks(2, skv, rkv, recv_sem.at[2])
        to_tasks(3, sqg, rqg, chunk_sem.at[y])

    front_row()
    lon_group_entered()
    pl.when(early)(send_rows)
    columns_entered()
    over_lat(0, xg.at[0], cxg.at[0], 48)
    over_lat(1, xg.at[1], cxg.at[1], 48)
    pl.when(jnp.logical_not(early))(send_rows)
    def fold(a, op):
        out = a[:8]
        for r in range(8, a.shape[0], 8):
            out = op(out, a[r : r + 8])
        return out

    def softmax_stats(tiles, key, value, qz, gz, s_ref, g_ref, bias):
        size = s_ref.shape[0] // tiles
        peak = None
        for t in range(tiles):
            s = dot(key(t), qz, NT)
            if bias is not None:
                s = s + bias(t)
            s_ref[t * size : t * size + size] = s
            top = fold(s, jnp.maximum)
            peak = top if peak is None else jnp.maximum(peak, top)
        peak = jnp.max(peak, axis=0, keepdims=True) * EXP_SCALE
        total = inner_sum = jnp.zeros((8, qz.shape[0]), F32)
        for t in range(tiles):
            at = slice(t * size, t * size + size)
            p = jnp.exp2(s_ref[at] * EXP_SCALE - peak)
            gp = dot(value(t), gz, NT)
            s_ref[at] = p
            g_ref[at] = gp
            total = total + fold(p, jnp.add)
            inner_sum = inner_sum + fold(p * gp, jnp.add)
        inv = 1.0 / jnp.sum(total, axis=0, keepdims=True)
        return inv, jnp.sum(inner_sum, axis=0, keepdims=True) * inv

    low = lax.broadcasted_iota(jnp.int32, (256, 128), 1) < 64
    head_of_lane = lax.broadcasted_iota(jnp.int32, (128, 256), 1) // 64

    def columns(half, i_in, i_out):
        arrived(i_in, cxg.at[half])
        got = cxg.at[half]
        tokens = natural(
            [
                jnp.concatenate(
                    [got[p * 48 : p * 48 + 32, :] for p in range(b * 8, b * 8 + 8)], axis=0
                )
                for b in range(2)
            ]
        )
        grads = [got[p * 48 + 32 : p * 48 + 48, :].astype(F32) for p in range(GROUP)]
        grads = jnp.concatenate(
            [
                jnp.concatenate([a[t * 8 : t * 8 + 8] for a in grads], axis=0) for t in range(2)
            ],
            axis=1,
        )
        q = dot(tokens, w[:, 256:512]).astype(BF).astype(F32)
        k = dot(tokens, w[:, 768:1024]).astype(BF)
        v = dot(tokens, w[:, 1280:1536]).astype(BF)
        k_t = k.astype(F32).T.astype(BF)

        def by_head(a):
            return jnp.concatenate(
                [jnp.where(head_of_lane == h, a, 0.0).astype(BF) for h in range(4)], axis=0
            )

        qz, gz = by_head(q), by_head(grads)
        s_ref, g_ref = css.at[half], cgs.at[half]
        inv, delta = softmax_stats(
            1, lambda t: k, lambda t: v, qz, gz, s_ref, g_ref, lambda t: mask[...]
        )
        weights = s_ref[...] * inv
        ds = (weights * (g_ref[...] - delta)).astype(BF)
        dk = (dot(ds, qz) * TEMPER).astype(BF)
        dv = dot(weights.astype(BF), gz).astype(BF)
        dq_t = jnp.concatenate(
            [dot(k_t[h * 64 : h * 64 + 64], ds[:, h * 128 : h * 128 + 128]) for h in range(4)],
            axis=0,
        )
        dq = (dq_t.T * TEMPER).astype(BF)
        part = (
            dot(dq, w[:, 256:512], NT) + dot(dk, w[:, 768:1024], NT) + dot(dv, w[:, 1280:1536], NT)
        )
        for p in range(GROUP):
            cpart[half, p * 32 : p * 32 + 32, :] = jnp.concatenate(
                [part[p * 8 : p * 8 + 8, t * 128 : t * 128 + 128] for t in range(4)], axis=0
            ).astype(BF)
        over_lat(i_out, cpart.at[half], cret.at[half], 32)

    def chunk_rows(dy, size):
        return pl.ds(pl.multiple_of(lax.rem(y + dy, 4) * size, size), size)

    def row_stats():
        arrived(2, rkv)
        keys_t = rkv[...].astype(F32).T[:64].astype(BF)
        for t in range(4):
            kt[t] = keys_t[:, t * 256 : t * 256 + 256]
        stats = []
        for c, dy in enumerate((0, 1, 3, 2)):
            rows = rqg.at[chunk_rows(dy, 256)]
            pltpu.make_async_copy(rows, rows, chunk_sem.at[lax.rem(y + dy, 4)]).wait()
            qg = rows[...].astype(F32)
            qgz[c, :256] = jnp.where(low, qg, 0.0).astype(BF)
            qgz[c, 256:] = jnp.where(low, 0.0, qg).astype(BF)

            def keys(t):
                return rkv[t * 128 : t * 128 + 128, :]

            stats.append(
                softmax_stats(8, keys, keys, qgz[c, :256], qgz[c, 256:], ss.at[c], gs.at[c], None)
            )
        return stats

    def row_grads(stats):
        dqt = [jnp.zeros((64, 256), F32) for _ in range(4)]
        half_scale = jnp.where(low, TEMPER, 1.0)
        for dy in (2, 1, 3, 0):
            at = lax.rem(y + dy, 4)
            rows = pl.ds(pl.multiple_of(at * 256, 256), 256)
            acc = jnp.zeros((256, 128), F32)
            for c in range(4):
                inv, delta = stats[c]
                weights = ss[c, rows] * inv
                ds = (weights * (gs[c, rows] - delta)).astype(BF)
                acc += dot(ds, qgz[c, :256]) + dot(weights.astype(BF), qgz[c, 256:])
                dqt[c] += dot(kt[at], ds)
            sendkv[rows, :] = (acc * half_scale).astype(BF)
            from_tasks(6, sendkv, retkv, 64, lon_peers[4 * ((2, 1, 3, 0).index(dy)) :][:4])
        pltpu.make_async_copy(block(sendkv, lon, 64), task(retkv, lon, 64), recv_sem.at[6]).start()
        for c, dy in ((3, 2), (1, 1), (2, 3), (0, 0)):
            dq = dqt[c].T * TEMPER
            packed = [
                jnp.concatenate([dq[i * 64 : i * 64 + 32], dq[i * 64 + 32 : i * 64 + 64]], axis=1)
                for i in range(4)
            ]
            sendq[chunk_rows(dy, 128), :] = jnp.concatenate(packed, axis=0).astype(BF)
            from_tasks(5, sendq, retq, 32, lon_peers[4 * ((2, 1, 3, 0).index(dy)) :][:4])
        pltpu.make_async_copy(block(sendq, lon, 32), task(retq, lon, 32), recv_sem.at[5]).start()

    rows_at = jnp.where(early, 0, 1)

    @pl.loop(0, 2)
    def _(i):
        @pl.when(i == rows_at)
        def _():
            row_grads(row_stats())

        @pl.when(i != rows_at)
        def _():
            columns(0, 0, 4)
            columns(1, 1, 7)


    def home(a):
        return lax.dot_general(
            perm[2], a, (((0,), (0,)), ((), ())), preferred_element_type=F32
        ).astype(BF)

    arrived(4, cret.at[0])
    arrived(7, cret.at[1])
    back = [cret[half].astype(F32) for half in range(2)]
    total = jnp.concatenate(
        [
            jnp.concatenate(
                [
                    back[half][p * 32 + t * 8 : p * 32 + t * 8 + 8]
                    for p in range(GROUP)
                    for half in range(2)
                ],
                axis=0,
            )
            for t in range(4)
        ],
        axis=1,
    )
    arrived(6, retkv)
    total += dot(home(jnp.concatenate([retkv[h] for h in range(4)], axis=1)), wkv[...], NT)
    arrived(5, retq)
    halves = [
        jnp.concatenate([retq[h][:, k * 64 : k * 64 + 64] for h in range(4)], axis=1)
        for k in range(2)
    ]
    dq = jnp.concatenate(
        [halves[k][la * 32 : la * 32 + 32] for la in range(4) for k in range(2)], axis=0
    )
    out_ref[...] = (total + dot(home(dq), w[:, :256], NT)).astype(BF)

    sent(0, cxg.at[0])
    sent(1, cxg.at[1])
    sent(2, rkv.at[pl.ds(0, 960)])
    sent(3, rqg.at[pl.ds(0, 960)])
    sent(4, cret.at[0])
    sent(7, cret.at[1])
    sent(5, sendq.at[pl.ds(0, 480)])
    sent(6, sendkv.at[pl.ds(0, 960)])


def rows_of_tiles(a):
    return a.reshape(64, 4, 4, 128).transpose(0, 2, 1, 3).reshape(1024, 128)


def per_device(fields, in_weight, out_weight, cotangent):
    shape = fields.shape

    def vm(*dims, dtype=BF):
        return pltpu.VMEM(dims, dtype)

    out = pl.pallas_call(
        kernel,
        out_shape=jax.ShapeDtypeStruct((256, 512), BF),
        in_specs=[pl.BlockSpec(memory_space=pl.ANY)] * 4,
        out_specs=pl.BlockSpec(memory_space=pltpu.VMEM),
        scratch_shapes=[
            vm(1024, 128), vm(512, 1536), vm(512, 512), vm(1024, 128),
            vm(3, 256, 256), vm(512, 512), vm(128, 512, dtype=F32),
            vm(4, 256, 128), vm(4, 256, 128), vm(1024, 128), vm(1024, 128), vm(4, 64, 256),
            vm(4, 512, 128), vm(1024, 128), vm(512, 128),
            vm(4, 256, 128), vm(4, 128, 128),
            vm(4, 1024, 256, dtype=F32), vm(4, 1024, 256, dtype=F32),
            vm(2, 768, 128), vm(2, 768, 128), vm(2, 512, 128), vm(2, 512, 128),
            vm(2, 128, 512, dtype=F32), vm(2, 128, 512, dtype=F32),
            pltpu.SemaphoreType.DMA((4,)),
            pltpu.SemaphoreType.DMA((8,)), pltpu.SemaphoreType.DMA((8,)),
            pltpu.SemaphoreType.DMA((4,)), pltpu.SemaphoreType.REGULAR((2,)),
        ],
        compiler_params=pltpu.CompilerParams(
            collective_id=0, has_side_effects=True, vmem_limit_bytes=40 * 2**20
        ),
        name="axial_grads",
    )(*(
        pltpu.with_memory_space_constraint(a, pltpu.HBM)
        for a in (rows_of_tiles(fields), in_weight, out_weight, rows_of_tiles(cotangent))
    ))
    return out.reshape(shape)


def solution(mesh):
    placed = (P("lon", "lat", None), P(), P(), P("lon", "lat", None))
    return jax.shard_map(
        per_device, mesh=mesh, in_specs=placed, out_specs=P("lon", "lat", None), check_vma=False
    )
```

```python
import math

import jax
import jax.numpy as jnp
from jax import lax
from jax.experimental import pallas as pl
from jax.experimental.pallas import tpu as pltpu
from jax.sharding import PartitionSpec as P

MESH = pl.DeviceIdType.MESH
BF = jnp.bfloat16
F32 = jnp.float32
NT = (((1,), (1,)), ((), ()))
NN = (((1,), (0,)), ((), ()))
TEMPER = 0.125
EXP_SCALE = TEMPER * math.log2(math.e)
GROUP = 16


def dot(a, b, dims=NN):
    return lax.dot_general(a, b, dims, preferred_element_type=F32)


def kernel(
    x_hbm, w_hbm, wo_hbm, c_hbm, out_ref,
    x, w, wo, cot, perm, wkv, mask,
    skv, sqg, rkv, rqg, kt, qgz, sendkv, sendq, retkv, retq, ss, gs,
    xg, cxg, cpart, cret, css, cgs,
    in_sem, send_sem, recv_sem, chunk_sem, mate_sem,
):
    lon = lax.axis_index("lon")
    lat = lax.axis_index("lat")
    my_l = lax.div(lon, 4)
    my_h = lax.rem(lon, 4)

    loads = [
        pltpu.make_async_copy(src, dst, in_sem.at[i])
        for i, (src, dst) in enumerate(((x_hbm, x), (c_hbm, cot), (wo_hbm, wo), (w_hbm, w)))
    ]
    for load in loads:
        load.start()

    z_lat = lax.rem(lat, 8)
    lat_peers = [
        x_hi * 8 + lax.rem(z_lat + dz, 8) for dz in (4, 3, 5, 2, 6, 1, 7, 0) for x_hi in (0, 1)
    ]
    y, x_lo, core = lax.div(lon, 4), lax.rem(lax.div(lon, 2), 2), lax.rem(lon, 2)
    beside = y * 4 + (1 - x_lo) * 2 + core
    lon_peers = [
        lax.rem(y + dy, 4) * 4
        + (x_lo if dx == 0 else 1 - x_lo) * 2
        + (core if dc == 0 else 1 - core)
        for dy in (2, 1, 3, 0)
        for dx in (1, 0)
        for dc in (1, 0)
        if (dy, dx, dc) != (0, 0, 0)
    ]

    barrier = pltpu.get_barrier_semaphore()
    mate = lon + 1 - 2 * core
    for p in lat_peers:
        pl.semaphore_signal(
            barrier, inc=1, device_id=(beside + 1 - core, p), device_id_type=MESH
        )
    for dy in (2, 1, 3, 0):
        for dx in (1, 0):
            chip = lax.rem(y + dy, 4) * 4 + (x_lo if dx == 0 else 1 - x_lo) * 2
            if (dy, dx) != (0, 0):
                pl.semaphore_signal(barrier, inc=1, device_id=(chip, lat), device_id_type=MESH)
            else:

                @pl.when(core == 1)
                def _():
                    pl.semaphore_signal(barrier, inc=1, device_id=(mate, lat), device_id_type=MESH)

    def lon_group_entered():
        @pl.when(core == 0)
        def _():
            pl.semaphore_wait(barrier, GROUP - 1)
            pl.semaphore_signal(mate_sem.at[0], inc=1, device_id=(mate, lat), device_id_type=MESH)

        @pl.when(core == 1)
        def _():
            pl.semaphore_wait(mate_sem.at[0], 1)

    def columns_entered():
        @pl.when(core == 1)
        def _():
            pl.semaphore_wait(barrier, 2 * GROUP)
            pl.semaphore_signal(mate_sem.at[1], inc=1, device_id=(mate, lat), device_id_type=MESH)

        @pl.when(core == 0)
        def _():
            pl.semaphore_wait(mate_sem.at[1], 1)

    def task(ref, p, rows):
        return ref.at[lax.rem(p, 4), pl.ds(pl.multiple_of(lax.div(p, 4) * rows, rows), rows)]

    def block(ref, p, rows):
        return ref.at[pl.ds(pl.multiple_of(p * rows, rows), rows)]

    def over_lat(i, src, dst, rows):
        for p in lat_peers:
            pltpu.make_async_remote_copy(
                src_ref=block(src, p, rows),
                dst_ref=block(dst, lat, rows),
                send_sem=send_sem.at[i],
                recv_sem=recv_sem.at[i],
                device_id=(beside, p),
                device_id_type=MESH,
            ).start()

    def to_tasks(i, src, dst, landed):
        for p in lon_peers:
            pltpu.make_async_remote_copy(
                src_ref=task(src, p, 64),
                dst_ref=block(dst, lon, 64),
                send_sem=send_sem.at[i],
                recv_sem=landed,
                device_id=(p, lat),
                device_id_type=MESH,
            ).start()
        pltpu.make_async_copy(task(src, lon, 64), block(dst, lon, 64), landed).start()

    def from_tasks(i, src, dst, rows, peers):
        for p in peers:
            pltpu.make_async_remote_copy(
                src_ref=block(src, p, rows),
                dst_ref=task(dst, lon, rows),
                send_sem=send_sem.at[i],
                recv_sem=recv_sem.at[i],
                device_id=(p, lat),
                device_id_type=MESH,
            ).start()

    def arrived(i, ref):
        pltpu.make_async_copy(ref, ref, recv_sem.at[i]).wait()

    def sent(i, ref):
        pltpu.make_async_copy(ref, ref, send_sem.at[i]).wait()

    row = lax.broadcasted_iota(jnp.int32, (256, 256), 0)
    col = lax.broadcasted_iota(jnp.int32, (256, 256), 1)
    tile, inner = row // 64, row % 64

    def onehot(at):
        return jnp.where(col == at, 1.0, 0.0).astype(BF)

    perm[0] = onehot((inner // 4) * 16 + tile * 4 + inner % 4)
    perm[1] = onehot((inner % 16) * 16 + tile * 4 + inner // 16)
    perm[2] = onehot((row % 64) * 4 + row // 64)
    row = lax.broadcasted_iota(jnp.int32, (128, 512), 0)
    col = lax.broadcasted_iota(jnp.int32, (128, 512), 1)
    mask[...] = jnp.where((row // 4) % 2 == (col // 4) % 2, 0.0, -1e30)

    def regroup(blocks, which):
        return dot(perm[which], jnp.concatenate(blocks, axis=1)).astype(BF)

    def natural(blocks):
        moved = regroup(blocks, 0)
        return jnp.concatenate(
            [
                jnp.concatenate(
                    [moved[t * 64 : t * 64 + 64, b * 128 : b * 128 + 128] for t in range(4)], axis=1
                )
                for b in range(len(blocks))
            ],
            axis=0,
        )

    def quarters(ref):
        return [ref[b * 256 : b * 256 + 256, :] for b in range(4)]

    def lat_major(blocks):
        moved = regroup(blocks, 1)
        return jnp.concatenate(
            [
                jnp.concatenate(
                    [
                        moved[t * 64 + la * 16 : t * 64 + la * 16 + 16, b * 128 : b * 128 + 128]
                        for t in range(4)
                    ],
                    axis=1,
                )
                for la in range(4)
                for b in range(4)
            ],
            axis=0,
        )

    loads[1].wait()
    loads[2].wait()
    g = dot(natural(quarters(cot)), wo[...], NT)
    loads[0].wait()
    for half in range(2):
        for p in range(GROUP):
            xg[half, p * 48 : p * 48 + 32, :] = x[p * 64 + half * 32 : p * 64 + half * 32 + 32, :]
            xg[half, p * 48 + 32 : p * 48 + 48, :] = jnp.concatenate(
                [
                    g[p * 16 + half * 8 : p * 16 + half * 8 + 8, 256 + t * 128 : 384 + t * 128]
                    for t in range(2)
                ],
                axis=0,
            ).astype(BF)

    def front_row():
        xp = lat_major(quarters(x))
        loads[3].wait()
        for h in range(4):
            wkv[:, h * 128 : h * 128 + 64] = w[:, 512 + h * 64 : 576 + h * 64]
            wkv[:, h * 128 + 64 : h * 128 + 128] = w[:, 1024 + h * 64 : 1088 + h * 64]
        kv = dot(xp, wkv[...]).astype(BF)
        g_row = dot(perm[2], g[:, :256].astype(BF))
        q = dot(xp, w[:, :256])
        for h in range(4):
            skv[h] = kv[:, h * 128 : h * 128 + 128]
            sqg[h] = jnp.concatenate(
                [q[:, h * 64 : h * 64 + 64], g_row[:, h * 64 : h * 64 + 64]], axis=1
            ).astype(BF)

    early = z_lat < 4

    front_row()
    lon_group_entered()
    @pl.when(early)
    def _():
        to_tasks(2, skv, rkv, recv_sem.at[2])
        to_tasks(3, sqg, rqg, chunk_sem.at[y])

    @pl.when(jnp.logical_not(early))
    def _():
        to_tasks(2, skv, rkv, recv_sem.at[2])

    columns_entered()
    over_lat(0, xg.at[0], cxg.at[0], 48)
    over_lat(1, xg.at[1], cxg.at[1], 48)
    @pl.when(jnp.logical_not(early))
    def _():
        to_tasks(3, sqg, rqg, chunk_sem.at[y])

    def fold(a, op):
        out = a[:8]
        for r in range(8, a.shape[0], 8):
            out = op(out, a[r : r + 8])
        return out

    def softmax_stats(tiles, key, value, qz, gz, s_ref, g_ref, bias):
        size = s_ref.shape[0] // tiles
        peak = None
        for t in range(tiles):
            s = dot(key(t), qz, NT)
            if bias is not None:
                s = s + bias(t)
            s_ref[t * size : t * size + size] = s
            top = fold(s, jnp.maximum)
            peak = top if peak is None else jnp.maximum(peak, top)
        peak = jnp.max(peak, axis=0, keepdims=True) * EXP_SCALE
        total = inner_sum = jnp.zeros((8, qz.shape[0]), F32)
        for t in range(tiles):
            at = slice(t * size, t * size + size)
            p = jnp.exp2(s_ref[at] * EXP_SCALE - peak)
            gp = dot(value(t), gz, NT)
            s_ref[at] = p
            g_ref[at] = gp
            total = total + fold(p, jnp.add)
            inner_sum = inner_sum + fold(p * gp, jnp.add)
        inv = 1.0 / jnp.sum(total, axis=0, keepdims=True)
        return inv, jnp.sum(inner_sum, axis=0, keepdims=True) * inv

    low = lax.broadcasted_iota(jnp.int32, (256, 128), 1) < 64
    head_of_lane = lax.broadcasted_iota(jnp.int32, (128, 256), 1) // 64

    def columns(half, i_in, i_out):
        arrived(i_in, cxg.at[half])
        got = cxg.at[half]
        tokens = natural(
            [
                jnp.concatenate(
                    [got[p * 48 : p * 48 + 32, :] for p in range(b * 8, b * 8 + 8)], axis=0
                )
                for b in range(2)
            ]
        )
        grads = [got[p * 48 + 32 : p * 48 + 48, :].astype(F32) for p in range(GROUP)]
        grads = jnp.concatenate(
            [
                jnp.concatenate([a[t * 8 : t * 8 + 8] for a in grads], axis=0) for t in range(2)
            ],
            axis=1,
        )
        q = dot(tokens, w[:, 256:512]).astype(BF).astype(F32)
        k = dot(tokens, w[:, 768:1024]).astype(BF)
        v = dot(tokens, w[:, 1280:1536]).astype(BF)
        k_t = k.astype(F32).T.astype(BF)

        def by_head(a):
            return jnp.concatenate(
                [jnp.where(head_of_lane == h, a, 0.0).astype(BF) for h in range(4)], axis=0
            )

        qz, gz = by_head(q), by_head(grads)
        s_ref, g_ref = css.at[half], cgs.at[half]
        inv, delta = softmax_stats(
            1, lambda t: k, lambda t: v, qz, gz, s_ref, g_ref, lambda t: mask[...]
        )
        weights = s_ref[...] * inv
        ds = (weights * (g_ref[...] - delta)).astype(BF)
        dk = (dot(ds, qz) * TEMPER).astype(BF)
        dv = dot(weights.astype(BF), gz).astype(BF)
        dq_t = jnp.concatenate(
            [dot(k_t[h * 64 : h * 64 + 64], ds[:, h * 128 : h * 128 + 128]) for h in range(4)],
            axis=0,
        )
        dq = (dq_t.T * TEMPER).astype(BF)
        part = (
            dot(dq, w[:, 256:512], NT) + dot(dk, w[:, 768:1024], NT) + dot(dv, w[:, 1280:1536], NT)
        )
        for p in range(GROUP):
            cpart[half, p * 32 : p * 32 + 32, :] = jnp.concatenate(
                [part[p * 8 : p * 8 + 8, t * 128 : t * 128 + 128] for t in range(4)], axis=0
            ).astype(BF)
        over_lat(i_out, cpart.at[half], cret.at[half], 32)

    def chunk_rows(dy, size):
        return pl.ds(pl.multiple_of(lax.rem(y + dy, 4) * size, size), size)

    def row_stats():
        arrived(2, rkv)
        keys_t = rkv[...].astype(F32).T[:64].astype(BF)
        for t in range(4):
            kt[t] = keys_t[:, t * 256 : t * 256 + 256]
        stats = []
        for c, dy in enumerate((0, 1, 3, 2)):
            rows = rqg.at[chunk_rows(dy, 256)]
            pltpu.make_async_copy(rows, rows, chunk_sem.at[lax.rem(y + dy, 4)]).wait()
            qg = rows[...].astype(F32)
            qgz[c, :256] = jnp.where(low, qg, 0.0).astype(BF)
            qgz[c, 256:] = jnp.where(low, 0.0, qg).astype(BF)

            def keys(t):
                return rkv[t * 128 : t * 128 + 128, :]

            stats.append(
                softmax_stats(8, keys, keys, qgz[c, :256], qgz[c, 256:], ss.at[c], gs.at[c], None)
            )
        return stats

    def row_grads(stats):
        dqt = [jnp.zeros((64, 256), F32) for _ in range(4)]
        half_scale = jnp.where(low, TEMPER, 1.0)
        for dy in (2, 1, 3, 0):
            at = lax.rem(y + dy, 4)
            rows = pl.ds(pl.multiple_of(at * 256, 256), 256)
            acc = jnp.zeros((256, 128), F32)
            for c in range(4):
                inv, delta = stats[c]
                weights = ss[c, rows] * inv
                ds = (weights * (gs[c, rows] - delta)).astype(BF)
                acc += dot(ds, qgz[c, :256]) + dot(weights.astype(BF), qgz[c, 256:])
                dqt[c] += dot(kt[at], ds)
            sendkv[rows, :] = (acc * half_scale).astype(BF)
            from_tasks(6, sendkv, retkv, 64, lon_peers[4 * ((2, 1, 3, 0).index(dy)) :][:4])
        pltpu.make_async_copy(block(sendkv, lon, 64), task(retkv, lon, 64), recv_sem.at[6]).start()
        for c, dy in ((3, 2), (1, 1), (2, 3), (0, 0)):
            dq = dqt[c].T * TEMPER
            packed = [
                jnp.concatenate([dq[i * 64 : i * 64 + 32], dq[i * 64 + 32 : i * 64 + 64]], axis=1)
                for i in range(4)
            ]
            sendq[chunk_rows(dy, 128), :] = jnp.concatenate(packed, axis=0).astype(BF)
            from_tasks(5, sendq, retq, 32, lon_peers[4 * ((2, 1, 3, 0).index(dy)) :][:4])
        pltpu.make_async_copy(block(sendq, lon, 32), task(retq, lon, 32), recv_sem.at[5]).start()

    rows_at = jnp.where(early, 0, 1)

    @pl.loop(0, 2)
    def _(i):
        @pl.when(i == rows_at)
        def _():
            row_grads(row_stats())

        @pl.when(i != rows_at)
        def _():
            columns(0, 0, 4)
            columns(1, 1, 7)


    def home(a):
        return lax.dot_general(
            perm[2], a, (((0,), (0,)), ((), ())), preferred_element_type=F32
        ).astype(BF)

    def column_result():
        arrived(4, cret.at[0])
        arrived(7, cret.at[1])
        back = [cret[half].astype(F32) for half in range(2)]
        return jnp.concatenate(
            [
                jnp.concatenate(
                    [
                        back[half][p * 32 + t * 8 : p * 32 + t * 8 + 8]
                        for p in range(GROUP)
                        for half in range(2)
                    ],
                    axis=0,
                )
                for t in range(4)
            ],
            axis=1,
        )

    def row_result(first):
        arrived(6, retkv)
        first += dot(home(jnp.concatenate([retkv[h] for h in range(4)], axis=1)), wkv[...], NT)
        arrived(5, retq)
        halves = [
            jnp.concatenate([retq[h][:, k * 64 : k * 64 + 64] for h in range(4)], axis=1)
            for k in range(2)
        ]
        dq = jnp.concatenate(
            [halves[k][la * 32 : la * 32 + 32] for la in range(4) for k in range(2)], axis=0
        )
        return first + dot(home(dq), w[:, :256], NT)

    @pl.when(early)
    def _():
        total = row_result(0.0)
        out_ref[...] = (total + column_result()).astype(BF)

    @pl.when(jnp.logical_not(early))
    def _():
        out_ref[...] = row_result(column_result()).astype(BF)

    sent(0, cxg.at[0])
    sent(1, cxg.at[1])
    sent(2, rkv.at[pl.ds(0, 960)])
    sent(3, rqg.at[pl.ds(0, 960)])
    sent(4, cret.at[0])
    sent(7, cret.at[1])
    sent(5, sendq.at[pl.ds(0, 480)])
    sent(6, sendkv.at[pl.ds(0, 960)])


def rows_of_tiles(a):
    return a.reshape(64, 4, 4, 128).transpose(0, 2, 1, 3).reshape(1024, 128)


def per_device(fields, in_weight, out_weight, cotangent):
    shape = fields.shape

    def vm(*dims, dtype=BF):
        return pltpu.VMEM(dims, dtype)

    out = pl.pallas_call(
        kernel,
        out_shape=jax.ShapeDtypeStruct((256, 512), BF),
        in_specs=[pl.BlockSpec(memory_space=pl.ANY)] * 4,
        out_specs=pl.BlockSpec(memory_space=pltpu.VMEM),
        scratch_shapes=[
            vm(1024, 128), vm(512, 1536), vm(512, 512), vm(1024, 128),
            vm(3, 256, 256), vm(512, 512), vm(128, 512, dtype=F32),
            vm(4, 256, 128), vm(4, 256, 128), vm(1024, 128), vm(1024, 128), vm(4, 64, 256),
            vm(4, 512, 128), vm(1024, 128), vm(512, 128),
            vm(4, 256, 128), vm(4, 128, 128),
            vm(4, 1024, 256, dtype=F32), vm(4, 1024, 256, dtype=F32),
            vm(2, 768, 128), vm(2, 768, 128), vm(2, 512, 128), vm(2, 512, 128),
            vm(2, 128, 512, dtype=F32), vm(2, 128, 512, dtype=F32),
            pltpu.SemaphoreType.DMA((4,)),
            pltpu.SemaphoreType.DMA((8,)), pltpu.SemaphoreType.DMA((8,)),
            pltpu.SemaphoreType.DMA((4,)), pltpu.SemaphoreType.REGULAR((2,)),
        ],
        compiler_params=pltpu.CompilerParams(
            collective_id=0, has_side_effects=True, vmem_limit_bytes=40 * 2**20
        ),
        name="axial_grads",
    )(*(
        pltpu.with_memory_space_constraint(a, pltpu.HBM)
        for a in (rows_of_tiles(fields), in_weight, out_weight, rows_of_tiles(cotangent))
    ))
    return out.reshape(shape)


def solution(mesh):
    placed = (P("lon", "lat", None), P(), P(), P("lon", "lat", None))
    return jax.shard_map(
        per_device, mesh=mesh, in_specs=placed, out_specs=P("lon", "lat", None), check_vma=False
    )
```

```python
import math

import jax
import jax.numpy as jnp
from jax import lax
from jax.experimental import pallas as pl
from jax.experimental.pallas import tpu as pltpu
from jax.sharding import PartitionSpec as P

MESH = pl.DeviceIdType.MESH
BF = jnp.bfloat16
F32 = jnp.float32
NT = (((1,), (1,)), ((), ()))
NN = (((1,), (0,)), ((), ()))
TEMPER = 0.125
EXP_SCALE = TEMPER * math.log2(math.e)
GROUP = 16


def dot(a, b, dims=NN):
    return lax.dot_general(a, b, dims, preferred_element_type=F32)


def kernel(
    x_hbm, w_hbm, wo_hbm, c_hbm, out_ref,
    x, w, wo, cot, perm, wkv, mask,
    skv, sqg, rkv, rqg, kt, qgz, sendkv, sendq, retkv, retq, ss, gs,
    xg, cxg, cpart, cret, css, cgs,
    in_sem, send_sem, recv_sem, chunk_sem, mate_sem,
):
    lon = lax.axis_index("lon")
    lat = lax.axis_index("lat")
    my_l = lax.div(lon, 4)
    my_h = lax.rem(lon, 4)

    loads = [
        pltpu.make_async_copy(src, dst, in_sem.at[i])
        for i, (src, dst) in enumerate(((x_hbm, x), (c_hbm, cot), (wo_hbm, wo), (w_hbm, w)))
    ]
    for load in loads:
        load.start()

    z_lat = lax.rem(lat, 8)
    lat_peers = [
        x_hi * 8 + lax.rem(z_lat + dz, 8) for x_hi in (0, 1) for dz in (4, 3, 5, 2, 6, 1, 7, 0)
    ]
    y, x_lo, core = lax.div(lon, 4), lax.rem(lax.div(lon, 2), 2), lax.rem(lon, 2)
    beside = y * 4 + (1 - x_lo) * 2 + core
    lon_peers = [
        lax.rem(y + dy, 4) * 4
        + (x_lo if dx == 0 else 1 - x_lo) * 2
        + (core if dc == 0 else 1 - core)
        for dy in (2, 1, 3, 0)
        for dx in (1, 0)
        for dc in (1, 0)
        if (dy, dx, dc) != (0, 0, 0)
    ]

    barrier = pltpu.get_barrier_semaphore()
    mate = lon + 1 - 2 * core
    for p in lat_peers:
        pl.semaphore_signal(
            barrier, inc=1, device_id=(beside + 1 - core, p), device_id_type=MESH
        )
    for dy in (2, 1, 3, 0):
        for dx in (1, 0):
            chip = lax.rem(y + dy, 4) * 4 + (x_lo if dx == 0 else 1 - x_lo) * 2
            if (dy, dx) != (0, 0):
                pl.semaphore_signal(barrier, inc=1, device_id=(chip, lat), device_id_type=MESH)
            else:

                @pl.when(core == 1)
                def _():
                    pl.semaphore_signal(barrier, inc=1, device_id=(mate, lat), device_id_type=MESH)

    def lon_group_entered():
        @pl.when(core == 0)
        def _():
            pl.semaphore_wait(barrier, GROUP - 1)
            pl.semaphore_signal(mate_sem.at[0], inc=1, device_id=(mate, lat), device_id_type=MESH)

        @pl.when(core == 1)
        def _():
            pl.semaphore_wait(mate_sem.at[0], 1)

    def columns_entered():
        @pl.when(core == 1)
        def _():
            pl.semaphore_wait(barrier, 2 * GROUP)
            pl.semaphore_signal(mate_sem.at[1], inc=1, device_id=(mate, lat), device_id_type=MESH)

        @pl.when(core == 0)
        def _():
            pl.semaphore_wait(mate_sem.at[1], 1)

    def task(ref, p, rows):
        return ref.at[lax.rem(p, 4), pl.ds(pl.multiple_of(lax.div(p, 4) * rows, rows), rows)]

    def block(ref, p, rows):
        return ref.at[pl.ds(pl.multiple_of(p * rows, rows), rows)]

    def over_lat(i, src, dst, rows):
        for p in lat_peers:
            pltpu.make_async_remote_copy(
                src_ref=block(src, p, rows),
                dst_ref=block(dst, lat, rows),
                send_sem=send_sem.at[i],
                recv_sem=recv_sem.at[i],
                device_id=(beside, p),
                device_id_type=MESH,
            ).start()

    def to_tasks(i, src, dst, landed):
        for p in lon_peers:
            pltpu.make_async_remote_copy(
                src_ref=task(src, p, 64),
                dst_ref=block(dst, lon, 64),
                send_sem=send_sem.at[i],
                recv_sem=landed,
                device_id=(p, lat),
                device_id_type=MESH,
            ).start()
        pltpu.make_async_copy(task(src, lon, 64), block(dst, lon, 64), landed).start()

    def from_tasks(i, src, dst, rows, peers):
        for p in peers:
            pltpu.make_async_remote_copy(
                src_ref=block(src, p, rows),
                dst_ref=task(dst, lon, rows),
                send_sem=send_sem.at[i],
                recv_sem=recv_sem.at[i],
                device_id=(p, lat),
                device_id_type=MESH,
            ).start()

    def arrived(i, ref):
        pltpu.make_async_copy(ref, ref, recv_sem.at[i]).wait()

    def sent(i, ref):
        pltpu.make_async_copy(ref, ref, send_sem.at[i]).wait()

    row = lax.broadcasted_iota(jnp.int32, (256, 256), 0)
    col = lax.broadcasted_iota(jnp.int32, (256, 256), 1)
    tile, inner = row // 64, row % 64

    def onehot(at):
        return jnp.where(col == at, 1.0, 0.0).astype(BF)

    perm[0] = onehot((inner // 4) * 16 + tile * 4 + inner % 4)
    perm[1] = onehot((inner % 16) * 16 + tile * 4 + inner // 16)
    perm[2] = onehot((row % 64) * 4 + row // 64)
    row = lax.broadcasted_iota(jnp.int32, (128, 512), 0)
    col = lax.broadcasted_iota(jnp.int32, (128, 512), 1)
    mask[...] = jnp.where((row // 4) % 2 == (col // 4) % 2, 0.0, -1e30)

    def regroup(blocks, which):
        return dot(perm[which], jnp.concatenate(blocks, axis=1)).astype(BF)

    def natural(blocks):
        moved = regroup(blocks, 0)
        return jnp.concatenate(
            [
                jnp.concatenate(
                    [moved[t * 64 : t * 64 + 64, b * 128 : b * 128 + 128] for t in range(4)], axis=1
                )
                for b in range(len(blocks))
            ],
            axis=0,
        )

    def quarters(ref):
        return [ref[b * 256 : b * 256 + 256, :] for b in range(4)]

    def lat_major(blocks):
        moved = regroup(blocks, 1)
        return jnp.concatenate(
            [
                jnp.concatenate(
                    [
                        moved[t * 64 + la * 16 : t * 64 + la * 16 + 16, b * 128 : b * 128 + 128]
                        for t in range(4)
                    ],
                    axis=1,
                )
                for la in range(4)
                for b in range(4)
            ],
            axis=0,
        )

    loads[1].wait()
    loads[2].wait()
    g = dot(natural(quarters(cot)), wo[...], NT)
    loads[0].wait()
    for half in range(2):
        for p in range(GROUP):
            xg[half, p * 48 : p * 48 + 32, :] = x[p * 64 + half * 32 : p * 64 + half * 32 + 32, :]
            xg[half, p * 48 + 32 : p * 48 + 48, :] = jnp.concatenate(
                [
                    g[p * 16 + half * 8 : p * 16 + half * 8 + 8, 256 + t * 128 : 384 + t * 128]
                    for t in range(2)
                ],
                axis=0,
            ).astype(BF)

    def front_row():
        xp = lat_major(quarters(x))
        loads[3].wait()
        for h in range(4):
            wkv[:, h * 128 : h * 128 + 64] = w[:, 512 + h * 64 : 576 + h * 64]
            wkv[:, h * 128 + 64 : h * 128 + 128] = w[:, 1024 + h * 64 : 1088 + h * 64]
        kv = dot(xp, wkv[...]).astype(BF)
        g_row = dot(perm[2], g[:, :256].astype(BF))
        q = dot(xp, w[:, :256])
        for h in range(4):
            skv[h] = kv[:, h * 128 : h * 128 + 128]
            sqg[h] = jnp.concatenate(
                [q[:, h * 64 : h * 64 + 64], g_row[:, h * 64 : h * 64 + 64]], axis=1
            ).astype(BF)

    early = z_lat < 4

    front_row()
    lon_group_entered()
    @pl.when(early)
    def _():
        to_tasks(2, skv, rkv, recv_sem.at[2])
        to_tasks(3, sqg, rqg, chunk_sem.at[y])

    @pl.when(jnp.logical_not(early))
    def _():
        to_tasks(2, skv, rkv, recv_sem.at[2])

    columns_entered()
    over_lat(0, xg.at[0], cxg.at[0], 48)
    over_lat(1, xg.at[1], cxg.at[1], 48)
    @pl.when(jnp.logical_not(early))
    def _():
        to_tasks(3, sqg, rqg, chunk_sem.at[y])

    def fold(a, op):
        out = a[:8]
        for r in range(8, a.shape[0], 8):
            out = op(out, a[r : r + 8])
        return out

    def softmax_stats(tiles, key, value, qz, gz, s_ref, g_ref, bias):
        size = s_ref.shape[0] // tiles
        peak = None
        for t in range(tiles):
            s = dot(key(t), qz, NT)
            if bias is not None:
                s = s + bias(t)
            s_ref[t * size : t * size + size] = s
            top = fold(s, jnp.maximum)
            peak = top if peak is None else jnp.maximum(peak, top)
        peak = jnp.max(peak, axis=0, keepdims=True) * EXP_SCALE
        total = inner_sum = jnp.zeros((8, qz.shape[0]), F32)
        for t in range(tiles):
            at = slice(t * size, t * size + size)
            p = jnp.exp2(s_ref[at] * EXP_SCALE - peak)
            gp = dot(value(t), gz, NT)
            s_ref[at] = p
            g_ref[at] = gp
            total = total + fold(p, jnp.add)
            inner_sum = inner_sum + fold(p * gp, jnp.add)
        inv = 1.0 / jnp.sum(total, axis=0, keepdims=True)
        return inv, jnp.sum(inner_sum, axis=0, keepdims=True) * inv

    low = lax.broadcasted_iota(jnp.int32, (256, 128), 1) < 64
    head_of_lane = lax.broadcasted_iota(jnp.int32, (128, 256), 1) // 64

    def columns(half, i_in, i_out):
        arrived(i_in, cxg.at[half])
        got = cxg.at[half]
        tokens = natural(
            [
                jnp.concatenate(
                    [got[p * 48 : p * 48 + 32, :] for p in range(b * 8, b * 8 + 8)], axis=0
                )
                for b in range(2)
            ]
        )
        grads = [got[p * 48 + 32 : p * 48 + 48, :].astype(F32) for p in range(GROUP)]
        grads = jnp.concatenate(
            [
                jnp.concatenate([a[t * 8 : t * 8 + 8] for a in grads], axis=0) for t in range(2)
            ],
            axis=1,
        )
        q = dot(tokens, w[:, 256:512]).astype(BF).astype(F32)
        k = dot(tokens, w[:, 768:1024]).astype(BF)
        v = dot(tokens, w[:, 1280:1536]).astype(BF)
        k_t = k.astype(F32).T.astype(BF)

        def by_head(a):
            return jnp.concatenate(
                [jnp.where(head_of_lane == h, a, 0.0).astype(BF) for h in range(4)], axis=0
            )

        qz, gz = by_head(q), by_head(grads)
        s_ref, g_ref = css.at[half], cgs.at[half]
        inv, delta = softmax_stats(
            1, lambda t: k, lambda t: v, qz, gz, s_ref, g_ref, lambda t: mask[...]
        )
        weights = s_ref[...] * inv
        ds = (weights * (g_ref[...] - delta)).astype(BF)
        dk = (dot(ds, qz) * TEMPER).astype(BF)
        dv = dot(weights.astype(BF), gz).astype(BF)
        dq_t = jnp.concatenate(
            [dot(k_t[h * 64 : h * 64 + 64], ds[:, h * 128 : h * 128 + 128]) for h in range(4)],
            axis=0,
        )
        dq = (dq_t.T * TEMPER).astype(BF)
        part = (
            dot(dq, w[:, 256:512], NT) + dot(dk, w[:, 768:1024], NT) + dot(dv, w[:, 1280:1536], NT)
        )
        for p in range(GROUP):
            cpart[half, p * 32 : p * 32 + 32, :] = jnp.concatenate(
                [part[p * 8 : p * 8 + 8, t * 128 : t * 128 + 128] for t in range(4)], axis=0
            ).astype(BF)
        over_lat(i_out, cpart.at[half], cret.at[half], 32)

    def chunk_rows(dy, size):
        return pl.ds(pl.multiple_of(lax.rem(y + dy, 4) * size, size), size)

    def row_stats():
        arrived(2, rkv)
        keys_t = rkv[...].astype(F32).T[:64].astype(BF)
        for t in range(4):
            kt[t] = keys_t[:, t * 256 : t * 256 + 256]
        stats = []
        for c, dy in enumerate((0, 1, 3, 2)):
            rows = rqg.at[chunk_rows(dy, 256)]
            pltpu.make_async_copy(rows, rows, chunk_sem.at[lax.rem(y + dy, 4)]).wait()
            qg = rows[...].astype(F32)
            qgz[c, :256] = jnp.where(low, qg, 0.0).astype(BF)
            qgz[c, 256:] = jnp.where(low, 0.0, qg).astype(BF)

            def keys(t):
                return rkv[t * 128 : t * 128 + 128, :]

            stats.append(
                softmax_stats(8, keys, keys, qgz[c, :256], qgz[c, 256:], ss.at[c], gs.at[c], None)
            )
        return stats

    def row_grads(stats):
        dqt = [jnp.zeros((64, 256), F32) for _ in range(4)]
        half_scale = jnp.where(low, TEMPER, 1.0)
        for dy in (2, 1, 3, 0):
            at = lax.rem(y + dy, 4)
            rows = pl.ds(pl.multiple_of(at * 256, 256), 256)
            acc = jnp.zeros((256, 128), F32)
            for c in range(4):
                inv, delta = stats[c]
                weights = ss[c, rows] * inv
                ds = (weights * (gs[c, rows] - delta)).astype(BF)
                acc += dot(ds, qgz[c, :256]) + dot(weights.astype(BF), qgz[c, 256:])
                dqt[c] += dot(kt[at], ds)
            sendkv[rows, :] = (acc * half_scale).astype(BF)
            from_tasks(6, sendkv, retkv, 64, lon_peers[4 * ((2, 1, 3, 0).index(dy)) :][:4])
        pltpu.make_async_copy(block(sendkv, lon, 64), task(retkv, lon, 64), recv_sem.at[6]).start()
        for c, dy in ((3, 2), (1, 1), (2, 3), (0, 0)):
            dq = dqt[c].T * TEMPER
            packed = [
                jnp.concatenate([dq[i * 64 : i * 64 + 32], dq[i * 64 + 32 : i * 64 + 64]], axis=1)
                for i in range(4)
            ]
            sendq[chunk_rows(dy, 128), :] = jnp.concatenate(packed, axis=0).astype(BF)
            from_tasks(5, sendq, retq, 32, lon_peers[4 * ((2, 1, 3, 0).index(dy)) :][:4])
        pltpu.make_async_copy(block(sendq, lon, 32), task(retq, lon, 32), recv_sem.at[5]).start()

    rows_at = jnp.where(early, 0, 1)

    @pl.loop(0, 2)
    def _(i):
        @pl.when(i == rows_at)
        def _():
            row_grads(row_stats())

        @pl.when(i != rows_at)
        def _():
            columns(0, 0, 4)
            columns(1, 1, 7)


    def home(a):
        return lax.dot_general(
            perm[2], a, (((0,), (0,)), ((), ())), preferred_element_type=F32
        ).astype(BF)

    def column_result():
        arrived(4, cret.at[0])
        arrived(7, cret.at[1])
        back = [cret[half].astype(F32) for half in range(2)]
        return jnp.concatenate(
            [
                jnp.concatenate(
                    [
                        back[half][p * 32 + t * 8 : p * 32 + t * 8 + 8]
                        for p in range(GROUP)
                        for half in range(2)
                    ],
                    axis=0,
                )
                for t in range(4)
            ],
            axis=1,
        )

    def row_result(first):
        arrived(6, retkv)
        first += dot(home(jnp.concatenate([retkv[h] for h in range(4)], axis=1)), wkv[...], NT)
        arrived(5, retq)
        halves = [
            jnp.concatenate([retq[h][:, k * 64 : k * 64 + 64] for h in range(4)], axis=1)
            for k in range(2)
        ]
        dq = jnp.concatenate(
            [halves[k][la * 32 : la * 32 + 32] for la in range(4) for k in range(2)], axis=0
        )
        return first + dot(home(dq), w[:, :256], NT)

    @pl.when(early)
    def _():
        total = row_result(0.0)
        out_ref[...] = (total + column_result()).astype(BF)

    @pl.when(jnp.logical_not(early))
    def _():
        out_ref[...] = row_result(column_result()).astype(BF)

    sent(0, cxg.at[0])
    sent(1, cxg.at[1])
    sent(2, rkv.at[pl.ds(0, 960)])
    sent(3, rqg.at[pl.ds(0, 960)])
    sent(4, cret.at[0])
    sent(7, cret.at[1])
    sent(5, sendq.at[pl.ds(0, 480)])
    sent(6, sendkv.at[pl.ds(0, 960)])


def rows_of_tiles(a):
    return a.reshape(64, 4, 4, 128).transpose(0, 2, 1, 3).reshape(1024, 128)


def per_device(fields, in_weight, out_weight, cotangent):
    shape = fields.shape

    def vm(*dims, dtype=BF):
        return pltpu.VMEM(dims, dtype)

    out = pl.pallas_call(
        kernel,
        out_shape=jax.ShapeDtypeStruct((256, 512), BF),
        in_specs=[pl.BlockSpec(memory_space=pl.ANY)] * 4,
        out_specs=pl.BlockSpec(memory_space=pltpu.VMEM),
        scratch_shapes=[
            vm(1024, 128), vm(512, 1536), vm(512, 512), vm(1024, 128),
            vm(3, 256, 256), vm(512, 512), vm(128, 512, dtype=F32),
            vm(4, 256, 128), vm(4, 256, 128), vm(1024, 128), vm(1024, 128), vm(4, 64, 256),
            vm(4, 512, 128), vm(1024, 128), vm(512, 128),
            vm(4, 256, 128), vm(4, 128, 128),
            vm(4, 1024, 256, dtype=F32), vm(4, 1024, 256, dtype=F32),
            vm(2, 768, 128), vm(2, 768, 128), vm(2, 512, 128), vm(2, 512, 128),
            vm(2, 128, 512, dtype=F32), vm(2, 128, 512, dtype=F32),
            pltpu.SemaphoreType.DMA((4,)),
            pltpu.SemaphoreType.DMA((8,)), pltpu.SemaphoreType.DMA((8,)),
            pltpu.SemaphoreType.DMA((4,)), pltpu.SemaphoreType.REGULAR((2,)),
        ],
        compiler_params=pltpu.CompilerParams(
            collective_id=0, has_side_effects=True, vmem_limit_bytes=40 * 2**20
        ),
        name="axial_grads",
    )(*(
        pltpu.with_memory_space_constraint(a, pltpu.HBM)
        for a in (rows_of_tiles(fields), in_weight, out_weight, rows_of_tiles(cotangent))
    ))
    return out.reshape(shape)


def solution(mesh):
    placed = (P("lon", "lat", None), P(), P(), P("lon", "lat", None))
    return jax.shard_map(
        per_device, mesh=mesh, in_specs=placed, out_specs=P("lon", "lat", None), check_vma=False
    )
```

```python
import math

import jax
import jax.numpy as jnp
from jax import lax
from jax.experimental import pallas as pl
from jax.experimental.pallas import tpu as pltpu
from jax.sharding import PartitionSpec as P

MESH = pl.DeviceIdType.MESH
BF = jnp.bfloat16
F32 = jnp.float32
NT = (((1,), (1,)), ((), ()))
NN = (((1,), (0,)), ((), ()))
TEMPER = 0.125
EXP_SCALE = TEMPER * math.log2(math.e)
GROUP = 16


def dot(a, b, dims=NN):
    return lax.dot_general(a, b, dims, preferred_element_type=F32)


def kernel(
    x_hbm, w_hbm, wo_hbm, c_hbm, out_ref,
    x, w, wo, cot, perm, wkv, mask,
    skv, sqg, rkv, rqg, kt, qgz, sendkv, sendq, retkv, retq, ss, gs,
    xg, cxg, cpart, cret, css, cgs,
    in_sem, send_sem, recv_sem, chunk_sem, mate_sem,
):
    lon = lax.axis_index("lon")
    lat = lax.axis_index("lat")
    my_l = lax.div(lon, 4)
    my_h = lax.rem(lon, 4)

    loads = [
        pltpu.make_async_copy(src, dst, in_sem.at[i])
        for i, (src, dst) in enumerate(((x_hbm, x), (c_hbm, cot), (wo_hbm, wo), (w_hbm, w)))
    ]
    for load in loads:
        load.start()

    z_lat = lax.rem(lat, 8)
    lat_peers = [
        x_hi * 8 + lax.rem(z_lat + dz, 8) for x_hi in (0, 1) for dz in (4, 3, 5, 2, 6, 1, 7, 0)
    ]
    y, x_lo, core = lax.div(lon, 4), lax.rem(lax.div(lon, 2), 2), lax.rem(lon, 2)
    beside = y * 4 + (1 - x_lo) * 2 + core
    lon_peers = [
        lax.rem(y + dy, 4) * 4
        + (x_lo if dx == 0 else 1 - x_lo) * 2
        + (core if dc == 0 else 1 - core)
        for dy in (2, 1, 3, 0)
        for dx in (1, 0)
        for dc in (1, 0)
        if (dy, dx, dc) != (0, 0, 0)
    ]

    barrier = pltpu.get_barrier_semaphore()
    mate = lon + 1 - 2 * core
    for p in lat_peers:
        pl.semaphore_signal(
            barrier, inc=1, device_id=(beside + 1 - core, p), device_id_type=MESH
        )
    for dy in (2, 1, 3, 0):
        for dx in (1, 0):
            chip = lax.rem(y + dy, 4) * 4 + (x_lo if dx == 0 else 1 - x_lo) * 2
            if (dy, dx) != (0, 0):
                pl.semaphore_signal(barrier, inc=1, device_id=(chip, lat), device_id_type=MESH)
            else:

                @pl.when(core == 1)
                def _():
                    pl.semaphore_signal(barrier, inc=1, device_id=(mate, lat), device_id_type=MESH)

    def lon_group_entered():
        @pl.when(core == 0)
        def _():
            pl.semaphore_wait(barrier, GROUP - 1)
            pl.semaphore_signal(mate_sem.at[0], inc=1, device_id=(mate, lat), device_id_type=MESH)

        @pl.when(core == 1)
        def _():
            pl.semaphore_wait(mate_sem.at[0], 1)

    def columns_entered():
        @pl.when(core == 1)
        def _():
            pl.semaphore_wait(barrier, 2 * GROUP)
            pl.semaphore_signal(mate_sem.at[1], inc=1, device_id=(mate, lat), device_id_type=MESH)

        @pl.when(core == 0)
        def _():
            pl.semaphore_wait(mate_sem.at[1], 1)

    def task(ref, p, rows):
        return ref.at[lax.rem(p, 4), pl.ds(pl.multiple_of(lax.div(p, 4) * rows, rows), rows)]

    def block(ref, p, rows):
        return ref.at[pl.ds(pl.multiple_of(p * rows, rows), rows)]

    def over_lat(i, src, dst, rows):
        for p in lat_peers:
            pltpu.make_async_remote_copy(
                src_ref=block(src, p, rows),
                dst_ref=block(dst, lat, rows),
                send_sem=send_sem.at[i],
                recv_sem=recv_sem.at[i],
                device_id=(beside, p),
                device_id_type=MESH,
            ).start()

    def to_tasks(i, src, dst, landed):
        for p in lon_peers:
            pltpu.make_async_remote_copy(
                src_ref=task(src, p, 64),
                dst_ref=block(dst, lon, 64),
                send_sem=send_sem.at[i],
                recv_sem=landed,
                device_id=(p, lat),
                device_id_type=MESH,
            ).start()
        pltpu.make_async_copy(task(src, lon, 64), block(dst, lon, 64), landed).start()

    def from_tasks(i, src, dst, rows, peers):
        for p in peers:
            pltpu.make_async_remote_copy(
                src_ref=block(src, p, rows),
                dst_ref=task(dst, lon, rows),
                send_sem=send_sem.at[i],
                recv_sem=recv_sem.at[i],
                device_id=(p, lat),
                device_id_type=MESH,
            ).start()

    def arrived(i, ref):
        pltpu.make_async_copy(ref, ref, recv_sem.at[i]).wait()

    def sent(i, ref):
        pltpu.make_async_copy(ref, ref, send_sem.at[i]).wait()

    row = lax.broadcasted_iota(jnp.int32, (256, 256), 0)
    col = lax.broadcasted_iota(jnp.int32, (256, 256), 1)
    tile, inner = row // 64, row % 64

    def onehot(at):
        return jnp.where(col == at, 1.0, 0.0).astype(BF)

    perm[0] = onehot((inner // 4) * 16 + tile * 4 + inner % 4)
    perm[1] = onehot((inner % 16) * 16 + tile * 4 + inner // 16)
    perm[2] = onehot((row % 64) * 4 + row // 64)
    row = lax.broadcasted_iota(jnp.int32, (128, 512), 0)
    col = lax.broadcasted_iota(jnp.int32, (128, 512), 1)
    mask[...] = jnp.where((row // 4) % 2 == (col // 4) % 2, 0.0, -1e30)

    def regroup(blocks, which):
        return dot(perm[which], jnp.concatenate(blocks, axis=1)).astype(BF)

    def natural(blocks):
        moved = regroup(blocks, 0)
        return jnp.concatenate(
            [
                jnp.concatenate(
                    [moved[t * 64 : t * 64 + 64, b * 128 : b * 128 + 128] for t in range(4)], axis=1
                )
                for b in range(len(blocks))
            ],
            axis=0,
        )

    def quarters(ref):
        return [ref[b * 256 : b * 256 + 256, :] for b in range(4)]

    def lat_major(blocks):
        moved = regroup(blocks, 1)
        return jnp.concatenate(
            [
                jnp.concatenate(
                    [
                        moved[t * 64 + la * 16 : t * 64 + la * 16 + 16, b * 128 : b * 128 + 128]
                        for t in range(4)
                    ],
                    axis=1,
                )
                for la in range(4)
                for b in range(4)
            ],
            axis=0,
        )

    loads[1].wait()
    loads[2].wait()
    g = dot(natural(quarters(cot)), wo[...], NT)
    loads[0].wait()
    for half in range(2):
        for p in range(GROUP):
            xg[half, p * 48 : p * 48 + 32, :] = x[p * 64 + half * 32 : p * 64 + half * 32 + 32, :]
            xg[half, p * 48 + 32 : p * 48 + 48, :] = jnp.concatenate(
                [
                    g[p * 16 + half * 8 : p * 16 + half * 8 + 8, 256 + t * 128 : 384 + t * 128]
                    for t in range(2)
                ],
                axis=0,
            ).astype(BF)

    def front_row():
        xp = lat_major(quarters(x))
        loads[3].wait()
        for h in range(4):
            wkv[:, h * 128 : h * 128 + 64] = w[:, 512 + h * 64 : 576 + h * 64]
            wkv[:, h * 128 + 64 : h * 128 + 128] = w[:, 1024 + h * 64 : 1088 + h * 64]
        kv = dot(xp, wkv[...]).astype(BF)
        g_row = dot(perm[2], g[:, :256].astype(BF))
        q = dot(xp, w[:, :256])
        for h in range(4):
            skv[h] = kv[:, h * 128 : h * 128 + 128]
            sqg[h] = jnp.concatenate(
                [q[:, h * 64 : h * 64 + 64], g_row[:, h * 64 : h * 64 + 64]], axis=1
            ).astype(BF)

    early = z_lat < 4

    front_row()
    lon_group_entered()
    @pl.when(early)
    def _():
        to_tasks(2, skv, rkv, recv_sem.at[2])
        to_tasks(3, sqg, rqg, chunk_sem.at[y])

    @pl.when(jnp.logical_not(early))
    def _():
        to_tasks(2, skv, rkv, recv_sem.at[2])

    columns_entered()
    over_lat(0, xg.at[0], cxg.at[0], 48)
    over_lat(1, xg.at[1], cxg.at[1], 48)
    @pl.when(jnp.logical_not(early))
    def _():
        to_tasks(3, sqg, rqg, chunk_sem.at[y])

    def fold(a, op):
        out = a[:8]
        for r in range(8, a.shape[0], 8):
            out = op(out, a[r : r + 8])
        return out

    def softmax_stats(tiles, key, value, qz, gz, s_ref, g_ref, bias):
        size = s_ref.shape[0] // tiles
        peak = None
        for t in range(tiles):
            s = dot(key(t), qz, NT)
            if bias is not None:
                s = s + bias(t)
            s_ref[t * size : t * size + size] = s
            top = fold(s, jnp.maximum)
            peak = top if peak is None else jnp.maximum(peak, top)
        peak = jnp.max(peak, axis=0, keepdims=True)
        total = inner_sum = jnp.zeros((8, qz.shape[0]), F32)
        for t in range(tiles):
            at = slice(t * size, t * size + size)
            p = jnp.exp2((s_ref[at] - peak) * EXP_SCALE)
            gp = dot(value(t), gz, NT)
            s_ref[at] = p
            g_ref[at] = gp
            total = total + fold(p, jnp.add)
            inner_sum = inner_sum + fold(p * gp, jnp.add)
        inv = 1.0 / jnp.sum(total, axis=0, keepdims=True)
        return inv, jnp.sum(inner_sum, axis=0, keepdims=True) * inv

    low = lax.broadcasted_iota(jnp.int32, (256, 128), 1) < 64
    head_of_lane = lax.broadcasted_iota(jnp.int32, (128, 256), 1) // 64

    def columns(half, i_in, i_out):
        arrived(i_in, cxg.at[half])
        got = cxg.at[half]
        tokens = natural(
            [
                jnp.concatenate(
                    [got[p * 48 : p * 48 + 32, :] for p in range(b * 8, b * 8 + 8)], axis=0
                )
                for b in range(2)
            ]
        )
        grads = [got[p * 48 + 32 : p * 48 + 48, :].astype(F32) for p in range(GROUP)]
        grads = jnp.concatenate(
            [
                jnp.concatenate([a[t * 8 : t * 8 + 8] for a in grads], axis=0) for t in range(2)
            ],
            axis=1,
        )
        q = dot(tokens, w[:, 256:512]).astype(BF).astype(F32)
        k = dot(tokens, w[:, 768:1024]).astype(BF)
        v = dot(tokens, w[:, 1280:1536]).astype(BF)
        k_t = k.astype(F32).T.astype(BF)

        def by_head(a):
            return jnp.concatenate(
                [jnp.where(head_of_lane == h, a, 0.0).astype(BF) for h in range(4)], axis=0
            )

        qz, gz = by_head(q), by_head(grads)
        s_ref, g_ref = css.at[half], cgs.at[half]
        inv, delta = softmax_stats(
            1, lambda t: k, lambda t: v, qz, gz, s_ref, g_ref, lambda t: mask[...]
        )
        weights = s_ref[...] * inv
        ds = (weights * (g_ref[...] - delta)).astype(BF)
        dk = (dot(ds, qz) * TEMPER).astype(BF)
        dv = dot(weights.astype(BF), gz).astype(BF)
        dq_t = jnp.concatenate(
            [dot(k_t[h * 64 : h * 64 + 64], ds[:, h * 128 : h * 128 + 128]) for h in range(4)],
            axis=0,
        )
        dq = (dq_t.T * TEMPER).astype(BF)
        part = (
            dot(dq, w[:, 256:512], NT) + dot(dk, w[:, 768:1024], NT) + dot(dv, w[:, 1280:1536], NT)
        )
        for p in range(GROUP):
            cpart[half, p * 32 : p * 32 + 32, :] = jnp.concatenate(
                [part[p * 8 : p * 8 + 8, t * 128 : t * 128 + 128] for t in range(4)], axis=0
            ).astype(BF)
        over_lat(i_out, cpart.at[half], cret.at[half], 32)

    def chunk_rows(dy, size):
        return pl.ds(pl.multiple_of(lax.rem(y + dy, 4) * size, size), size)

    def row_stats():
        arrived(2, rkv)
        keys_t = rkv[...].astype(F32).T[:64].astype(BF)
        for t in range(4):
            kt[t] = keys_t[:, t * 256 : t * 256 + 256]
        stats = []
        for c, dy in enumerate((0, 1, 3, 2)):
            rows = rqg.at[chunk_rows(dy, 256)]
            pltpu.make_async_copy(rows, rows, chunk_sem.at[lax.rem(y + dy, 4)]).wait()
            qg = rows[...].astype(F32)
            qgz[c, :256] = jnp.where(low, qg, 0.0).astype(BF)
            qgz[c, 256:] = jnp.where(low, 0.0, qg).astype(BF)

            def keys(t):
                return rkv[t * 128 : t * 128 + 128, :]

            stats.append(
                softmax_stats(8, keys, keys, qgz[c, :256], qgz[c, 256:], ss.at[c], gs.at[c], None)
            )
        return stats

    def row_grads(stats):
        dqt = [jnp.zeros((64, 256), F32) for _ in range(4)]
        half_scale = jnp.where(low, TEMPER, 1.0)
        for dy in (2, 1, 3, 0):
            at = lax.rem(y + dy, 4)
            rows = pl.ds(pl.multiple_of(at * 256, 256), 256)
            acc = jnp.zeros((256, 128), F32)
            for c in range(4):
                inv, delta = stats[c]
                weights = ss[c, rows] * inv
                ds = (weights * (gs[c, rows] - delta)).astype(BF)
                acc += dot(ds, qgz[c, :256]) + dot(weights.astype(BF), qgz[c, 256:])
                dqt[c] += dot(kt[at], ds)
            sendkv[rows, :] = (acc * half_scale).astype(BF)
            from_tasks(6, sendkv, retkv, 64, lon_peers[4 * ((2, 1, 3, 0).index(dy)) :][:4])
        pltpu.make_async_copy(block(sendkv, lon, 64), task(retkv, lon, 64), recv_sem.at[6]).start()
        for c, dy in ((3, 2), (1, 1), (2, 3), (0, 0)):
            dq = dqt[c].T * TEMPER
            packed = [
                jnp.concatenate([dq[i * 64 : i * 64 + 32], dq[i * 64 + 32 : i * 64 + 64]], axis=1)
                for i in range(4)
            ]
            sendq[chunk_rows(dy, 128), :] = jnp.concatenate(packed, axis=0).astype(BF)
            from_tasks(5, sendq, retq, 32, lon_peers[4 * ((2, 1, 3, 0).index(dy)) :][:4])
        pltpu.make_async_copy(block(sendq, lon, 32), task(retq, lon, 32), recv_sem.at[5]).start()

    rows_at = jnp.where(early, 0, 1)

    @pl.loop(0, 2)
    def _(i):
        @pl.when(i == rows_at)
        def _():
            row_grads(row_stats())

        @pl.when(i != rows_at)
        def _():
            columns(0, 0, 4)
            columns(1, 1, 7)


    def home(a):
        return lax.dot_general(
            perm[2], a, (((0,), (0,)), ((), ())), preferred_element_type=F32
        ).astype(BF)

    def column_result():
        arrived(4, cret.at[0])
        arrived(7, cret.at[1])
        back = [cret[half].astype(F32) for half in range(2)]
        return jnp.concatenate(
            [
                jnp.concatenate(
                    [
                        back[half][p * 32 + t * 8 : p * 32 + t * 8 + 8]
                        for p in range(GROUP)
                        for half in range(2)
                    ],
                    axis=0,
                )
                for t in range(4)
            ],
            axis=1,
        )

    def row_result(first):
        arrived(6, retkv)
        first += dot(home(jnp.concatenate([retkv[h] for h in range(4)], axis=1)), wkv[...], NT)
        arrived(5, retq)
        halves = [
            jnp.concatenate([retq[h][:, k * 64 : k * 64 + 64] for h in range(4)], axis=1)
            for k in range(2)
        ]
        dq = jnp.concatenate(
            [halves[k][la * 32 : la * 32 + 32] for la in range(4) for k in range(2)], axis=0
        )
        return first + dot(home(dq), w[:, :256], NT)

    @pl.when(early)
    def _():
        total = row_result(0.0)
        out_ref[...] = (total + column_result()).astype(BF)

    @pl.when(jnp.logical_not(early))
    def _():
        out_ref[...] = row_result(column_result()).astype(BF)

    sent(0, cxg.at[0])
    sent(1, cxg.at[1])
    sent(2, rkv.at[pl.ds(0, 960)])
    sent(3, rqg.at[pl.ds(0, 960)])
    sent(4, cret.at[0])
    sent(7, cret.at[1])
    sent(5, sendq.at[pl.ds(0, 480)])
    sent(6, sendkv.at[pl.ds(0, 960)])


def rows_of_tiles(a):
    return a.reshape(64, 4, 4, 128).transpose(0, 2, 1, 3).reshape(1024, 128)


def per_device(fields, in_weight, out_weight, cotangent):
    shape = fields.shape

    def vm(*dims, dtype=BF):
        return pltpu.VMEM(dims, dtype)

    out = pl.pallas_call(
        kernel,
        out_shape=jax.ShapeDtypeStruct((256, 512), BF),
        in_specs=[pl.BlockSpec(memory_space=pl.ANY)] * 4,
        out_specs=pl.BlockSpec(memory_space=pltpu.VMEM),
        scratch_shapes=[
            vm(1024, 128), vm(512, 1536), vm(512, 512), vm(1024, 128),
            vm(3, 256, 256), vm(512, 512), vm(128, 512, dtype=F32),
            vm(4, 256, 128), vm(4, 256, 128), vm(1024, 128), vm(1024, 128), vm(4, 64, 256),
            vm(4, 512, 128), vm(1024, 128), vm(512, 128),
            vm(4, 256, 128), vm(4, 128, 128),
            vm(4, 1024, 256, dtype=F32), vm(4, 1024, 256, dtype=F32),
            vm(2, 768, 128), vm(2, 768, 128), vm(2, 512, 128), vm(2, 512, 128),
            vm(2, 128, 512, dtype=F32), vm(2, 128, 512, dtype=F32),
            pltpu.SemaphoreType.DMA((4,)),
            pltpu.SemaphoreType.DMA((8,)), pltpu.SemaphoreType.DMA((8,)),
            pltpu.SemaphoreType.DMA((4,)), pltpu.SemaphoreType.REGULAR((2,)),
        ],
        compiler_params=pltpu.CompilerParams(
            collective_id=0, has_side_effects=True, vmem_limit_bytes=40 * 2**20
        ),
        name="axial_grads",
    )(*(
        pltpu.with_memory_space_constraint(a, pltpu.HBM)
        for a in (rows_of_tiles(fields), in_weight, out_weight, rows_of_tiles(cotangent))
    ))
    return out.reshape(shape)


def solution(mesh):
    placed = (P("lon", "lat", None), P(), P(), P("lon", "lat", None))
    return jax.shard_map(
        per_device, mesh=mesh, in_specs=placed, out_specs=P("lon", "lat", None), check_vma=False
    )
```

```python
import math

import jax
import jax.numpy as jnp
from jax import lax
from jax.experimental import pallas as pl
from jax.experimental.pallas import tpu as pltpu
from jax.sharding import PartitionSpec as P

MESH = pl.DeviceIdType.MESH
BF = jnp.bfloat16
F32 = jnp.float32
NT = (((1,), (1,)), ((), ()))
NN = (((1,), (0,)), ((), ()))
TEMPER = 0.125
EXP_SCALE = TEMPER * math.log2(math.e)
GROUP = 16


def dot(a, b, dims=NN):
    return lax.dot_general(a, b, dims, preferred_element_type=F32)


def kernel(
    x_hbm, w_hbm, wo_hbm, c_hbm, out_ref,
    x, w, wo, cot, perm, wkv, mask,
    skv, sqg, rkv, rqg, kt, qgz, sendkv, sendq, retkv, retq, ss, gs,
    xg, cxg, cpart, cret, css, cgs,
    in_sem, send_sem, recv_sem, chunk_sem, mate_sem,
):
    lon = lax.axis_index("lon")
    lat = lax.axis_index("lat")
    my_l = lax.div(lon, 4)
    my_h = lax.rem(lon, 4)

    z_lat = lax.rem(lat, 8)
    lat_peers = [
        x_hi * 8 + lax.rem(z_lat + dz, 8) for x_hi in (0, 1) for dz in (4, 3, 5, 2, 6, 1, 7, 0)
    ]
    y, x_lo, core = lax.div(lon, 4), lax.rem(lax.div(lon, 2), 2), lax.rem(lon, 2)
    beside = y * 4 + (1 - x_lo) * 2 + core
    lon_peers = [
        lax.rem(y + dy, 4) * 4
        + (x_lo if dx == 0 else 1 - x_lo) * 2
        + (core if dc == 0 else 1 - core)
        for dy in (2, 1, 3, 0)
        for dx in (1, 0)
        for dc in (1, 0)
        if (dy, dx, dc) != (0, 0, 0)
    ]

    barrier = pltpu.get_barrier_semaphore()
    mate = lon + 1 - 2 * core
    for p in lat_peers:
        pl.semaphore_signal(
            barrier, inc=1, device_id=(beside + 1 - core, p), device_id_type=MESH
        )
    for dy in (2, 1, 3, 0):
        for dx in (1, 0):
            chip = lax.rem(y + dy, 4) * 4 + (x_lo if dx == 0 else 1 - x_lo) * 2
            if (dy, dx) != (0, 0):
                pl.semaphore_signal(barrier, inc=1, device_id=(chip, lat), device_id_type=MESH)
            else:

                @pl.when(core == 1)
                def _():
                    pl.semaphore_signal(barrier, inc=1, device_id=(mate, lat), device_id_type=MESH)

    loads = [
        pltpu.make_async_copy(src, dst, in_sem.at[i])
        for i, (src, dst) in enumerate(((x_hbm, x), (c_hbm, cot), (wo_hbm, wo), (w_hbm, w)))
    ]
    for load in loads:
        load.start()

    def lon_group_entered():
        @pl.when(core == 0)
        def _():
            pl.semaphore_wait(barrier, GROUP - 1)
            pl.semaphore_signal(mate_sem.at[0], inc=1, device_id=(mate, lat), device_id_type=MESH)

        @pl.when(core == 1)
        def _():
            pl.semaphore_wait(mate_sem.at[0], 1)

    def columns_entered():
        @pl.when(core == 1)
        def _():
            pl.semaphore_wait(barrier, 2 * GROUP)
            pl.semaphore_signal(mate_sem.at[1], inc=1, device_id=(mate, lat), device_id_type=MESH)

        @pl.when(core == 0)
        def _():
            pl.semaphore_wait(mate_sem.at[1], 1)

    def task(ref, p, rows):
        return ref.at[lax.rem(p, 4), pl.ds(pl.multiple_of(lax.div(p, 4) * rows, rows), rows)]

    def block(ref, p, rows):
        return ref.at[pl.ds(pl.multiple_of(p * rows, rows), rows)]

    def over_lat(i, src, dst, rows, peers):
        for p in peers:
            pltpu.make_async_remote_copy(
                src_ref=block(src, p, rows),
                dst_ref=block(dst, lat, rows),
                send_sem=send_sem.at[i],
                recv_sem=recv_sem.at[i],
                device_id=(beside, p),
                device_id_type=MESH,
            ).start()

    def to_tasks(i, src, dst, landed):
        for p in lon_peers:
            pltpu.make_async_remote_copy(
                src_ref=task(src, p, 64),
                dst_ref=block(dst, lon, 64),
                send_sem=send_sem.at[i],
                recv_sem=landed,
                device_id=(p, lat),
                device_id_type=MESH,
            ).start()
        pltpu.make_async_copy(task(src, lon, 64), block(dst, lon, 64), landed).start()

    def from_tasks(i, src, dst, rows, peers):
        for p in peers:
            pltpu.make_async_remote_copy(
                src_ref=block(src, p, rows),
                dst_ref=task(dst, lon, rows),
                send_sem=send_sem.at[i],
                recv_sem=recv_sem.at[i],
                device_id=(p, lat),
                device_id_type=MESH,
            ).start()

    def arrived(i, ref):
        pltpu.make_async_copy(ref, ref, recv_sem.at[i]).wait()

    def sent(i, ref):
        pltpu.make_async_copy(ref, ref, send_sem.at[i]).wait()

    row = lax.broadcasted_iota(jnp.int32, (256, 256), 0)
    col = lax.broadcasted_iota(jnp.int32, (256, 256), 1)
    tile, inner = row // 64, row % 64

    def onehot(at):
        return jnp.where(col == at, 1.0, 0.0).astype(BF)

    perm[0] = onehot((inner // 4) * 16 + tile * 4 + inner % 4)
    perm[1] = onehot((inner % 16) * 16 + tile * 4 + inner // 16)
    perm[2] = onehot((row % 64) * 4 + row // 64)
    row = lax.broadcasted_iota(jnp.int32, (128, 512), 0)
    col = lax.broadcasted_iota(jnp.int32, (128, 512), 1)
    mask[...] = jnp.where((row // 4) % 2 == (col // 4) % 2, 0.0, -1e30)

    def regroup(blocks, which):
        return dot(perm[which], jnp.concatenate(blocks, axis=1)).astype(BF)

    def natural(blocks):
        moved = regroup(blocks, 0)
        return jnp.concatenate(
            [
                jnp.concatenate(
                    [moved[t * 64 : t * 64 + 64, b * 128 : b * 128 + 128] for t in range(4)], axis=1
                )
                for b in range(len(blocks))
            ],
            axis=0,
        )

    def quarters(ref):
        return [ref[b * 256 : b * 256 + 256, :] for b in range(4)]

    def lat_major(blocks):
        moved = regroup(blocks, 1)
        return jnp.concatenate(
            [
                jnp.concatenate(
                    [
                        moved[t * 64 + la * 16 : t * 64 + la * 16 + 16, b * 128 : b * 128 + 128]
                        for t in range(4)
                    ],
                    axis=1,
                )
                for la in range(4)
                for b in range(4)
            ],
            axis=0,
        )

    loads[1].wait()
    loads[2].wait()
    g = dot(natural(quarters(cot)), wo[...], NT)
    loads[0].wait()
    for half in range(2):
        for p in range(GROUP):
            xg[half, p * 48 : p * 48 + 32, :] = x[p * 64 + half * 32 : p * 64 + half * 32 + 32, :]
            xg[half, p * 48 + 32 : p * 48 + 48, :] = jnp.concatenate(
                [
                    g[p * 16 + half * 8 : p * 16 + half * 8 + 8, 256 + t * 128 : 384 + t * 128]
                    for t in range(2)
                ],
                axis=0,
            ).astype(BF)

    def front_row():
        xp = lat_major(quarters(x))
        loads[3].wait()
        for h in range(4):
            wkv[:, h * 128 : h * 128 + 64] = w[:, 512 + h * 64 : 576 + h * 64]
            wkv[:, h * 128 + 64 : h * 128 + 128] = w[:, 1024 + h * 64 : 1088 + h * 64]
        kv = dot(xp, wkv[...]).astype(BF)
        g_row = dot(perm[2], g[:, :256].astype(BF))
        q = dot(xp, w[:, :256])
        for h in range(4):
            skv[h] = kv[:, h * 128 : h * 128 + 128]
            sqg[h] = jnp.concatenate(
                [q[:, h * 64 : h * 64 + 64], g_row[:, h * 64 : h * 64 + 64]], axis=1
            ).astype(BF)

    early = z_lat < 4

    front_row()
    lon_group_entered()
    @pl.when(early)
    def _():
        to_tasks(2, skv, rkv, recv_sem.at[2])
        to_tasks(3, sqg, rqg, chunk_sem.at[y])

    @pl.when(jnp.logical_not(early))
    def _():
        to_tasks(2, skv, rkv, recv_sem.at[2])

    columns_entered()
    over_lat(0, xg.at[0], cxg.at[0], 48, lat_peers)
    over_lat(1, xg.at[1], cxg.at[1], 48, lat_peers)
    @pl.when(jnp.logical_not(early))
    def _():
        to_tasks(3, sqg, rqg, chunk_sem.at[y])

    def fold(a, op):
        out = a[:8]
        for r in range(8, a.shape[0], 8):
            out = op(out, a[r : r + 8])
        return out

    def softmax_stats(tiles, key, value, qz, gz, s_ref, g_ref, bias):
        size = s_ref.shape[0] // tiles
        peak = None
        for t in range(tiles):
            s = dot(key(t), qz, NT)
            if bias is not None:
                s = s + bias(t)
            s_ref[t * size : t * size + size] = s
            top = fold(s, jnp.maximum)
            peak = top if peak is None else jnp.maximum(peak, top)
        peak = jnp.max(peak, axis=0, keepdims=True)
        total = inner_sum = jnp.zeros((8, qz.shape[0]), F32)
        for t in range(tiles):
            at = slice(t * size, t * size + size)
            p = jnp.exp2((s_ref[at] - peak) * EXP_SCALE)
            gp = dot(value(t), gz, NT)
            s_ref[at] = p
            g_ref[at] = gp
            total = total + fold(p, jnp.add)
            inner_sum = inner_sum + fold(p * gp, jnp.add)
        inv = 1.0 / jnp.sum(total, axis=0, keepdims=True)
        return inv, jnp.sum(inner_sum, axis=0, keepdims=True) * inv

    low = lax.broadcasted_iota(jnp.int32, (256, 128), 1) < 64
    head_of_lane = lax.broadcasted_iota(jnp.int32, (128, 256), 1) // 64

    def columns(half, i_in, i_out):
        arrived(i_in, cxg.at[half])
        got = cxg.at[half]
        tokens = natural(
            [
                jnp.concatenate(
                    [got[p * 48 : p * 48 + 32, :] for p in range(b * 8, b * 8 + 8)], axis=0
                )
                for b in range(2)
            ]
        )
        grads = [got[p * 48 + 32 : p * 48 + 48, :].astype(F32) for p in range(GROUP)]
        grads = jnp.concatenate(
            [
                jnp.concatenate([a[t * 8 : t * 8 + 8] for a in grads], axis=0) for t in range(2)
            ],
            axis=1,
        )
        q = dot(tokens, w[:, 256:512]).astype(BF).astype(F32)
        k = dot(tokens, w[:, 768:1024]).astype(BF)
        v = dot(tokens, w[:, 1280:1536]).astype(BF)
        k_t = k.astype(F32).T.astype(BF)

        def by_head(a):
            return jnp.concatenate(
                [jnp.where(head_of_lane == h, a, 0.0).astype(BF) for h in range(4)], axis=0
            )

        qz, gz = by_head(q), by_head(grads)
        s_ref, g_ref = css.at[half], cgs.at[half]
        inv, delta = softmax_stats(
            1, lambda t: k, lambda t: v, qz, gz, s_ref, g_ref, lambda t: mask[...]
        )
        weights = s_ref[...] * inv
        ds = (weights * (g_ref[...] - delta)).astype(BF)
        dk = (dot(ds, qz) * TEMPER).astype(BF)
        dv = dot(weights.astype(BF), gz).astype(BF)
        dq_t = jnp.concatenate(
            [dot(k_t[h * 64 : h * 64 + 64], ds[:, h * 128 : h * 128 + 128]) for h in range(4)],
            axis=0,
        )
        dq = (dq_t.T * TEMPER).astype(BF)
        part = (
            dot(dq, w[:, 256:512], NT) + dot(dk, w[:, 768:1024], NT) + dot(dv, w[:, 1280:1536], NT)
        )
        for p in range(GROUP):
            cpart[half, p * 32 : p * 32 + 32, :] = jnp.concatenate(
                [part[p * 8 : p * 8 + 8, t * 128 : t * 128 + 128] for t in range(4)], axis=0
            ).astype(BF)
        over_lat(i_out, cpart.at[half], cret.at[half], 32, range(GROUP))

    def chunk_rows(dy, size):
        return pl.ds(pl.multiple_of(lax.rem(y + dy, 4) * size, size), size)

    def row_stats():
        arrived(2, rkv)
        keys_t = rkv[...].astype(F32).T[:64].astype(BF)
        for t in range(4):
            kt[t] = keys_t[:, t * 256 : t * 256 + 256]
        stats = []
        for c, dy in enumerate((0, 1, 3, 2)):
            rows = rqg.at[chunk_rows(dy, 256)]
            pltpu.make_async_copy(rows, rows, chunk_sem.at[lax.rem(y + dy, 4)]).wait()
            qg = rows[...].astype(F32)
            qgz[c, :256] = jnp.where(low, qg, 0.0).astype(BF)
            qgz[c, 256:] = jnp.where(low, 0.0, qg).astype(BF)

            def keys(t):
                return rkv[t * 128 : t * 128 + 128, :]

            stats.append(
                softmax_stats(8, keys, keys, qgz[c, :256], qgz[c, 256:], ss.at[c], gs.at[c], None)
            )
        return stats

    def row_grads(stats):
        dqt = [jnp.zeros((64, 256), F32) for _ in range(4)]
        half_scale = jnp.where(low, TEMPER, 1.0)
        for dy in (2, 1, 3, 0):
            at = lax.rem(y + dy, 4)
            rows = pl.ds(pl.multiple_of(at * 256, 256), 256)
            acc = jnp.zeros((256, 128), F32)
            for c in range(4):
                inv, delta = stats[c]
                weights = ss[c, rows] * inv
                ds = (weights * (gs[c, rows] - delta)).astype(BF)
                acc += dot(ds, qgz[c, :256]) + dot(weights.astype(BF), qgz[c, 256:])
                dqt[c] += dot(kt[at], ds)
            sendkv[rows, :] = (acc * half_scale).astype(BF)
            from_tasks(6, sendkv, retkv, 64, lon_peers[4 * ((2, 1, 3, 0).index(dy)) :][:4])
        pltpu.make_async_copy(block(sendkv, lon, 64), task(retkv, lon, 64), recv_sem.at[6]).start()
        for c, dy in ((3, 2), (1, 1), (2, 3), (0, 0)):
            dq = dqt[c].T * TEMPER
            packed = [
                jnp.concatenate([dq[i * 64 : i * 64 + 32], dq[i * 64 + 32 : i * 64 + 64]], axis=1)
                for i in range(4)
            ]
            sendq[chunk_rows(dy, 128), :] = jnp.concatenate(packed, axis=0).astype(BF)
            from_tasks(5, sendq, retq, 32, lon_peers[4 * ((2, 1, 3, 0).index(dy)) :][:4])
        pltpu.make_async_copy(block(sendq, lon, 32), task(retq, lon, 32), recv_sem.at[5]).start()

    rows_at = jnp.where(early, 0, 1)

    @pl.loop(0, 2)
    def _(i):
        @pl.when(i == rows_at)
        def _():
            row_grads(row_stats())

        @pl.when(i != rows_at)
        def _():
            columns(0, 0, 4)
            columns(1, 1, 7)


    def home(a):
        return lax.dot_general(
            perm[2], a, (((0,), (0,)), ((), ())), preferred_element_type=F32
        ).astype(BF)

    def column_result():
        arrived(4, cret.at[0])
        arrived(7, cret.at[1])
        back = [cret[half].astype(F32) for half in range(2)]
        return jnp.concatenate(
            [
                jnp.concatenate(
                    [
                        back[half][p * 32 + t * 8 : p * 32 + t * 8 + 8]
                        for p in range(GROUP)
                        for half in range(2)
                    ],
                    axis=0,
                )
                for t in range(4)
            ],
            axis=1,
        )

    def row_result(first):
        arrived(6, retkv)
        first += dot(home(jnp.concatenate([retkv[h] for h in range(4)], axis=1)), wkv[...], NT)
        arrived(5, retq)
        halves = [
            jnp.concatenate([retq[h][:, k * 64 : k * 64 + 64] for h in range(4)], axis=1)
            for k in range(2)
        ]
        dq = jnp.concatenate(
            [halves[k][la * 32 : la * 32 + 32] for la in range(4) for k in range(2)], axis=0
        )
        return first + dot(home(dq), w[:, :256], NT)

    @pl.when(early)
    def _():
        total = row_result(0.0)
        out_ref[...] = (total + column_result()).astype(BF)

    @pl.when(jnp.logical_not(early))
    def _():
        out_ref[...] = row_result(column_result()).astype(BF)

    sent(0, cxg.at[0])
    sent(1, cxg.at[1])
    sent(2, rkv.at[pl.ds(0, 960)])
    sent(3, rqg.at[pl.ds(0, 960)])
    sent(4, cret.at[0])
    sent(7, cret.at[1])
    sent(5, sendq.at[pl.ds(0, 480)])
    sent(6, sendkv.at[pl.ds(0, 960)])


def rows_of_tiles(a):
    return a.reshape(64, 4, 4, 128).transpose(0, 2, 1, 3).reshape(1024, 128)


def per_device(fields, in_weight, out_weight, cotangent):
    shape = fields.shape

    def vm(*dims, dtype=BF):
        return pltpu.VMEM(dims, dtype)

    out = pl.pallas_call(
        kernel,
        out_shape=jax.ShapeDtypeStruct((256, 512), BF),
        in_specs=[pl.BlockSpec(memory_space=pl.ANY)] * 4,
        out_specs=pl.BlockSpec(memory_space=pltpu.VMEM),
        scratch_shapes=[
            vm(1024, 128), vm(512, 1536), vm(512, 512), vm(1024, 128),
            vm(3, 256, 256), vm(512, 512), vm(128, 512, dtype=F32),
            vm(4, 256, 128), vm(4, 256, 128), vm(1024, 128), vm(1024, 128), vm(4, 64, 256),
            vm(4, 512, 128), vm(1024, 128), vm(512, 128),
            vm(4, 256, 128), vm(4, 128, 128),
            vm(4, 1024, 256, dtype=F32), vm(4, 1024, 256, dtype=F32),
            vm(2, 768, 128), vm(2, 768, 128), vm(2, 512, 128), vm(2, 512, 128),
            vm(2, 128, 512, dtype=F32), vm(2, 128, 512, dtype=F32),
            pltpu.SemaphoreType.DMA((4,)),
            pltpu.SemaphoreType.DMA((8,)), pltpu.SemaphoreType.DMA((8,)),
            pltpu.SemaphoreType.DMA((4,)), pltpu.SemaphoreType.REGULAR((2,)),
        ],
        compiler_params=pltpu.CompilerParams(
            collective_id=0, has_side_effects=True, vmem_limit_bytes=40 * 2**20
        ),
        name="axial_grads",
    )(*(
        pltpu.with_memory_space_constraint(a, pltpu.HBM)
        for a in (rows_of_tiles(fields), in_weight, out_weight, rows_of_tiles(cotangent))
    ))
    return out.reshape(shape)


def solution(mesh):
    placed = (P("lon", "lat", None), P(), P(), P("lon", "lat", None))
    return jax.shard_map(
        per_device, mesh=mesh, in_specs=placed, out_specs=P("lon", "lat", None), check_vma=False
    )
```

```python
import math

import jax
import jax.numpy as jnp
from jax import lax
from jax.experimental import pallas as pl
from jax.experimental.pallas import tpu as pltpu
from jax.sharding import PartitionSpec as P

MESH = pl.DeviceIdType.MESH
BF = jnp.bfloat16
F32 = jnp.float32
NT = (((1,), (1,)), ((), ()))
NN = (((1,), (0,)), ((), ()))
TEMPER = 0.125
EXP_SCALE = TEMPER * math.log2(math.e)
GROUP = 16


def dot(a, b, dims=NN):
    return lax.dot_general(a, b, dims, preferred_element_type=F32)


def kernel(
    x_hbm, w_hbm, wo_hbm, c_hbm, out_ref,
    x, w, wo, cot, perm, wkv, mask,
    skv, sqg, rkv, rqg, kt, qgz, sendkv, sendq, retkv, retq, ss, gs,
    xg, cxg, cpart, cret, css, cgs,
    in_sem, send_sem, recv_sem, chunk_sem, mate_sem,
):
    lon = lax.axis_index("lon")
    lat = lax.axis_index("lat")
    my_l = lax.div(lon, 4)
    my_h = lax.rem(lon, 4)

    loads = [
        pltpu.make_async_copy(src, dst, in_sem.at[i])
        for i, (src, dst) in enumerate(((x_hbm, x), (c_hbm, cot), (wo_hbm, wo), (w_hbm, w)))
    ]
    for load in loads:
        load.start()

    z_lat = lax.rem(lat, 8)
    lat_peers = [
        x_hi * 8 + lax.rem(z_lat + dz, 8) for x_hi in (0, 1) for dz in (4, 3, 5, 2, 6, 1, 7, 0)
    ]
    y, x_lo, core = lax.div(lon, 4), lax.rem(lax.div(lon, 2), 2), lax.rem(lon, 2)
    beside = y * 4 + (1 - x_lo) * 2 + core
    lon_peers = [
        lax.rem(y + dy, 4) * 4
        + (x_lo if dx == 0 else 1 - x_lo) * 2
        + (core if dc == 0 else 1 - core)
        for dy in (2, 1, 3, 0)
        for dx in (1, 0)
        for dc in (1, 0)
        if (dy, dx, dc) != (0, 0, 0)
    ]

    barrier = pltpu.get_barrier_semaphore()
    mate = lon + 1 - 2 * core
    for p in lat_peers:
        pl.semaphore_signal(
            barrier, inc=1, device_id=(beside + 1 - core, p), device_id_type=MESH
        )
    for dy in (2, 1, 3, 0):
        for dx in (1, 0):
            chip = lax.rem(y + dy, 4) * 4 + (x_lo if dx == 0 else 1 - x_lo) * 2
            if (dy, dx) != (0, 0):
                pl.semaphore_signal(barrier, inc=1, device_id=(chip, lat), device_id_type=MESH)
            else:

                @pl.when(core == 1)
                def _():
                    pl.semaphore_signal(barrier, inc=1, device_id=(mate, lat), device_id_type=MESH)

    def lon_group_entered():
        @pl.when(core == 0)
        def _():
            pl.semaphore_wait(barrier, GROUP - 1)
            pl.semaphore_signal(mate_sem.at[0], inc=1, device_id=(mate, lat), device_id_type=MESH)

        @pl.when(core == 1)
        def _():
            pl.semaphore_wait(mate_sem.at[0], 1)

    def columns_entered():
        @pl.when(core == 1)
        def _():
            pl.semaphore_wait(barrier, 2 * GROUP)
            pl.semaphore_signal(mate_sem.at[1], inc=1, device_id=(mate, lat), device_id_type=MESH)

        @pl.when(core == 0)
        def _():
            pl.semaphore_wait(mate_sem.at[1], 1)

    def task(ref, p, rows):
        return ref.at[lax.rem(p, 4), pl.ds(pl.multiple_of(lax.div(p, 4) * rows, rows), rows)]

    def block(ref, p, rows):
        return ref.at[pl.ds(pl.multiple_of(p * rows, rows), rows)]

    def over_lat(i, src, dst, rows):
        for p in lat_peers:
            pltpu.make_async_remote_copy(
                src_ref=block(src, p, rows),
                dst_ref=block(dst, lat, rows),
                send_sem=send_sem.at[i],
                recv_sem=recv_sem.at[i],
                device_id=(beside, p),
                device_id_type=MESH,
            ).start()

    def to_tasks(i, src, dst, landed):
        for p in lon_peers:
            pltpu.make_async_remote_copy(
                src_ref=task(src, p, 64),
                dst_ref=block(dst, lon, 64),
                send_sem=send_sem.at[i],
                recv_sem=landed,
                device_id=(p, lat),
                device_id_type=MESH,
            ).start()
        pltpu.make_async_copy(task(src, lon, 64), block(dst, lon, 64), landed).start()

    def from_tasks(i, src, dst, rows, peers):
        for p in peers:
            pltpu.make_async_remote_copy(
                src_ref=block(src, p, rows),
                dst_ref=task(dst, lon, rows),
                send_sem=send_sem.at[i],
                recv_sem=recv_sem.at[i],
                device_id=(p, lat),
                device_id_type=MESH,
            ).start()

    def arrived(i, ref):
        pltpu.make_async_copy(ref, ref, recv_sem.at[i]).wait()

    def sent(i, ref):
        pltpu.make_async_copy(ref, ref, send_sem.at[i]).wait()

    row = lax.broadcasted_iota(jnp.int32, (256, 256), 0)
    col = lax.broadcasted_iota(jnp.int32, (256, 256), 1)
    tile, inner = row // 64, row % 64

    def onehot(at):
        return jnp.where(col == at, 1.0, 0.0).astype(BF)

    perm[0] = onehot((inner // 4) * 16 + tile * 4 + inner % 4)
    perm[1] = onehot((inner % 16) * 16 + tile * 4 + inner // 16)
    perm[2] = onehot((row % 64) * 4 + row // 64)
    row = lax.broadcasted_iota(jnp.int32, (128, 512), 0)
    col = lax.broadcasted_iota(jnp.int32, (128, 512), 1)
    mask[...] = jnp.where((row // 4) % 2 == (col // 4) % 2, 0.0, -1e30)

    def regroup(blocks, which):
        return dot(perm[which], jnp.concatenate(blocks, axis=1)).astype(BF)

    def natural(blocks):
        moved = regroup(blocks, 0)
        return jnp.concatenate(
            [
                jnp.concatenate(
                    [moved[t * 64 : t * 64 + 64, b * 128 : b * 128 + 128] for t in range(4)], axis=1
                )
                for b in range(len(blocks))
            ],
            axis=0,
        )

    def quarters(ref):
        return [ref[b * 256 : b * 256 + 256, :] for b in range(4)]

    def lat_major(blocks):
        moved = regroup(blocks, 1)
        return jnp.concatenate(
            [
                jnp.concatenate(
                    [
                        moved[t * 64 + la * 16 : t * 64 + la * 16 + 16, b * 128 : b * 128 + 128]
                        for t in range(4)
                    ],
                    axis=1,
                )
                for la in range(4)
                for b in range(4)
            ],
            axis=0,
        )

    loads[1].wait()
    loads[2].wait()
    g = dot(natural(quarters(cot)), wo[...], NT)
    loads[0].wait()
    for half in range(2):
        for p in range(GROUP):
            xg[half, p * 48 : p * 48 + 32, :] = x[p * 64 + half * 32 : p * 64 + half * 32 + 32, :]
            xg[half, p * 48 + 32 : p * 48 + 48, :] = jnp.concatenate(
                [
                    g[p * 16 + half * 8 : p * 16 + half * 8 + 8, 256 + t * 128 : 384 + t * 128]
                    for t in range(2)
                ],
                axis=0,
            ).astype(BF)

    def front_row():
        xp = lat_major(quarters(x))
        loads[3].wait()
        for h in range(4):
            wkv[:, h * 128 : h * 128 + 64] = w[:, 512 + h * 64 : 576 + h * 64]
            wkv[:, h * 128 + 64 : h * 128 + 128] = w[:, 1024 + h * 64 : 1088 + h * 64]
        kv = dot(xp, wkv[...]).astype(BF)
        g_row = dot(perm[2], g[:, :256].astype(BF))
        q = dot(xp, w[:, :256])
        for h in range(4):
            skv[h] = kv[:, h * 128 : h * 128 + 128]
            sqg[h] = jnp.concatenate(
                [q[:, h * 64 : h * 64 + 64], g_row[:, h * 64 : h * 64 + 64]], axis=1
            ).astype(BF)

    early = z_lat < 4

    front_row()
    lon_group_entered()
    @pl.when(early)
    def _():
        to_tasks(2, skv, rkv, recv_sem.at[2])
        to_tasks(3, sqg, rqg, chunk_sem.at[y])

    @pl.when(jnp.logical_not(early))
    def _():
        to_tasks(2, skv, rkv, recv_sem.at[2])

    columns_entered()
    over_lat(0, xg.at[0], cxg.at[0], 48)
    over_lat(1, xg.at[1], cxg.at[1], 48)
    @pl.when(jnp.logical_not(early))
    def _():
        to_tasks(3, sqg, rqg, chunk_sem.at[y])

    def fold(a, op):
        out = a[:8]
        for r in range(8, a.shape[0], 8):
            out = op(out, a[r : r + 8])
        return out

    def softmax_stats(tiles, key, value, qz, gz, s_ref, g_ref, bias):
        size = s_ref.shape[0] // tiles
        peak = None
        for t in range(tiles):
            s = dot(key(t), qz, NT)
            if bias is not None:
                s = s + bias(t)
            s_ref[t * size : t * size + size] = s
            top = fold(s, jnp.maximum)
            peak = top if peak is None else jnp.maximum(peak, top)
        peak = jnp.max(peak, axis=0, keepdims=True)
        total = inner_sum = jnp.zeros((8, qz.shape[0]), F32)
        for t in range(tiles):
            at = slice(t * size, t * size + size)
            p = jnp.exp2((s_ref[at] - peak) * EXP_SCALE)
            gp = dot(value(t), gz, NT)
            s_ref[at] = p
            g_ref[at] = gp
            total = total + fold(p, jnp.add)
            inner_sum = inner_sum + fold(p * gp, jnp.add)
        inv = 1.0 / jnp.sum(total, axis=0, keepdims=True)
        return inv, jnp.sum(inner_sum, axis=0, keepdims=True) * inv

    low = lax.broadcasted_iota(jnp.int32, (256, 128), 1) < 64
    head_of_lane = lax.broadcasted_iota(jnp.int32, (128, 256), 1) // 64

    def columns(half, i_in, i_out):
        arrived(i_in, cxg.at[half])
        got = cxg.at[half]
        tokens = natural(
            [
                jnp.concatenate(
                    [got[p * 48 : p * 48 + 32, :] for p in range(b * 8, b * 8 + 8)], axis=0
                )
                for b in range(2)
            ]
        )
        grads = [got[p * 48 + 32 : p * 48 + 48, :].astype(F32) for p in range(GROUP)]
        grads = jnp.concatenate(
            [
                jnp.concatenate([a[t * 8 : t * 8 + 8] for a in grads], axis=0) for t in range(2)
            ],
            axis=1,
        )
        q = dot(tokens, w[:, 256:512]).astype(BF).astype(F32)
        k = dot(tokens, w[:, 768:1024]).astype(BF)
        v = dot(tokens, w[:, 1280:1536]).astype(BF)
        k_t = k.astype(F32).T.astype(BF)

        def by_head(a):
            return jnp.concatenate(
                [jnp.where(head_of_lane == h, a, 0.0).astype(BF) for h in range(4)], axis=0
            )

        qz, gz = by_head(q), by_head(grads)
        s_ref, g_ref = css.at[half], cgs.at[half]
        inv, delta = softmax_stats(
            1, lambda t: k, lambda t: v, qz, gz, s_ref, g_ref, lambda t: mask[...]
        )
        weights = s_ref[...] * inv
        ds = (weights * (g_ref[...] - delta)).astype(BF)
        dk = (dot(ds, qz) * TEMPER).astype(BF)
        dv = dot(weights.astype(BF), gz).astype(BF)
        dq_t = jnp.concatenate(
            [dot(k_t[h * 64 : h * 64 + 64], ds[:, h * 128 : h * 128 + 128]) for h in range(4)],
            axis=0,
        )
        dq = (dq_t.T * TEMPER).astype(BF)
        part = (
            dot(dq, w[:, 256:512], NT) + dot(dk, w[:, 768:1024], NT) + dot(dv, w[:, 1280:1536], NT)
        )
        for p in range(GROUP):
            cpart[half, p * 32 : p * 32 + 32, :] = jnp.concatenate(
                [part[p * 8 : p * 8 + 8, t * 128 : t * 128 + 128] for t in range(4)], axis=0
            ).astype(BF)
        over_lat(i_out, cpart.at[half], cret.at[half], 32)

    def row_keys():
        arrived(2, rkv)
        keys_t = rkv[...].astype(F32).T[:64].astype(BF)
        for t in range(4):
            kt[t] = keys_t[:, t * 256 : t * 256 + 256]

    def chunk_rows(dy, size):
        return pl.ds(pl.multiple_of(lax.rem(y + dy, 4) * size, size), size)

    def row_stats():
        stats = []
        for c, dy in enumerate((0, 1, 3, 2)):
            rows = rqg.at[chunk_rows(dy, 256)]
            pltpu.make_async_copy(rows, rows, chunk_sem.at[lax.rem(y + dy, 4)]).wait()
            qg = rows[...].astype(F32)
            qgz[c, :256] = jnp.where(low, qg, 0.0).astype(BF)
            qgz[c, 256:] = jnp.where(low, 0.0, qg).astype(BF)

            def keys(t):
                return rkv[t * 128 : t * 128 + 128, :]

            stats.append(
                softmax_stats(8, keys, keys, qgz[c, :256], qgz[c, 256:], ss.at[c], gs.at[c], None)
            )
        return stats

    def row_grads(stats):
        dqt = [jnp.zeros((64, 256), F32) for _ in range(4)]
        half_scale = jnp.where(low, TEMPER, 1.0)
        for dy in (2, 1, 3, 0):
            at = lax.rem(y + dy, 4)
            rows = pl.ds(pl.multiple_of(at * 256, 256), 256)
            acc = jnp.zeros((256, 128), F32)
            for c in range(4):
                inv, delta = stats[c]
                weights = ss[c, rows] * inv
                ds = (weights * (gs[c, rows] - delta)).astype(BF)
                acc += dot(ds, qgz[c, :256]) + dot(weights.astype(BF), qgz[c, 256:])
                dqt[c] += dot(kt[at], ds)
            sendkv[rows, :] = (acc * half_scale).astype(BF)
            from_tasks(6, sendkv, retkv, 64, lon_peers[4 * ((2, 1, 3, 0).index(dy)) :][:4])
        pltpu.make_async_copy(block(sendkv, lon, 64), task(retkv, lon, 64), recv_sem.at[6]).start()
        for c, dy in ((3, 2), (1, 1), (2, 3), (0, 0)):
            dq = dqt[c].T * TEMPER
            packed = [
                jnp.concatenate([dq[i * 64 : i * 64 + 32], dq[i * 64 + 32 : i * 64 + 64]], axis=1)
                for i in range(4)
            ]
            sendq[chunk_rows(dy, 128), :] = jnp.concatenate(packed, axis=0).astype(BF)
            from_tasks(5, sendq, retq, 32, lon_peers[4 * ((2, 1, 3, 0).index(dy)) :][:4])
        pltpu.make_async_copy(block(sendq, lon, 32), task(retq, lon, 32), recv_sem.at[5]).start()

    rows_at = jnp.where(early, 0, 1)

    @pl.loop(0, 2)
    def _(i):
        @pl.when(i == rows_at)
        def _():
            pl.when(early)(row_keys)
            row_grads(row_stats())

        @pl.when(i != rows_at)
        def _():
            columns(0, 0, 4)
            pl.when(jnp.logical_not(early))(row_keys)
            columns(1, 1, 7)


    def home(a):
        return lax.dot_general(
            perm[2], a, (((0,), (0,)), ((), ())), preferred_element_type=F32
        ).astype(BF)

    def column_result():
        arrived(4, cret.at[0])
        arrived(7, cret.at[1])
        back = [cret[half].astype(F32) for half in range(2)]
        return jnp.concatenate(
            [
                jnp.concatenate(
                    [
                        back[half][p * 32 + t * 8 : p * 32 + t * 8 + 8]
                        for p in range(GROUP)
                        for half in range(2)
                    ],
                    axis=0,
                )
                for t in range(4)
            ],
            axis=1,
        )

    def row_result(first):
        arrived(6, retkv)
        first += dot(home(jnp.concatenate([retkv[h] for h in range(4)], axis=1)), wkv[...], NT)
        arrived(5, retq)
        halves = [
            jnp.concatenate([retq[h][:, k * 64 : k * 64 + 64] for h in range(4)], axis=1)
            for k in range(2)
        ]
        dq = jnp.concatenate(
            [halves[k][la * 32 : la * 32 + 32] for la in range(4) for k in range(2)], axis=0
        )
        return first + dot(home(dq), w[:, :256], NT)

    @pl.when(early)
    def _():
        total = row_result(0.0)
        out_ref[...] = (total + column_result()).astype(BF)

    @pl.when(jnp.logical_not(early))
    def _():
        out_ref[...] = row_result(column_result()).astype(BF)

    sent(0, cxg.at[0])
    sent(1, cxg.at[1])
    sent(2, rkv.at[pl.ds(0, 960)])
    sent(3, rqg.at[pl.ds(0, 960)])
    sent(4, cret.at[0])
    sent(7, cret.at[1])
    sent(5, sendq.at[pl.ds(0, 480)])
    sent(6, sendkv.at[pl.ds(0, 960)])


def rows_of_tiles(a):
    return a.reshape(64, 4, 4, 128).transpose(0, 2, 1, 3).reshape(1024, 128)


def per_device(fields, in_weight, out_weight, cotangent):
    shape = fields.shape

    def vm(*dims, dtype=BF):
        return pltpu.VMEM(dims, dtype)

    out = pl.pallas_call(
        kernel,
        out_shape=jax.ShapeDtypeStruct((256, 512), BF),
        in_specs=[pl.BlockSpec(memory_space=pl.ANY)] * 4,
        out_specs=pl.BlockSpec(memory_space=pltpu.VMEM),
        scratch_shapes=[
            vm(1024, 128), vm(512, 1536), vm(512, 512), vm(1024, 128),
            vm(3, 256, 256), vm(512, 512), vm(128, 512, dtype=F32),
            vm(4, 256, 128), vm(4, 256, 128), vm(1024, 128), vm(1024, 128), vm(4, 64, 256),
            vm(4, 512, 128), vm(1024, 128), vm(512, 128),
            vm(4, 256, 128), vm(4, 128, 128),
            vm(4, 1024, 256, dtype=F32), vm(4, 1024, 256, dtype=F32),
            vm(2, 768, 128), vm(2, 768, 128), vm(2, 512, 128), vm(2, 512, 128),
            vm(2, 128, 512, dtype=F32), vm(2, 128, 512, dtype=F32),
            pltpu.SemaphoreType.DMA((4,)),
            pltpu.SemaphoreType.DMA((8,)), pltpu.SemaphoreType.DMA((8,)),
            pltpu.SemaphoreType.DMA((4,)), pltpu.SemaphoreType.REGULAR((2,)),
        ],
        compiler_params=pltpu.CompilerParams(
            collective_id=0, has_side_effects=True, vmem_limit_bytes=40 * 2**20
        ),
        name="axial_grads",
    )(*(
        pltpu.with_memory_space_constraint(a, pltpu.HBM)
        for a in (rows_of_tiles(fields), in_weight, out_weight, rows_of_tiles(cotangent))
    ))
    return out.reshape(shape)


def solution(mesh):
    placed = (P("lon", "lat", None), P(), P(), P("lon", "lat", None))
    return jax.shard_map(
        per_device, mesh=mesh, in_specs=placed, out_specs=P("lon", "lat", None), check_vma=False
    )
```
